128 devices in a mesh: req: 4 (over x), grp: 32 (over z, y, core).
Axes of the slice: x: 4, y: 4, z: 4, core: 2. Of those that a mesh axis runs over, the one named last changes fastest.
Arguments:
- rows_in: bfloat16 [4, 160, 8192], P('req'), may hold values from -6 to 6
- norm_gain: float32 [8192], replicated, may hold values from 0.5 to 1.5
- w_query: bfloat16 [8192, 8192], P(None, 'grp'), may hold values from -0.0625 to 0.0625
- w_keyval: bfloat16 [8192, 2048], P(None, 'grp'), may hold values from -0.0625 to 0.0625
- w_out: bfloat16 [8192, 8192], P(None, 'grp'), may hold values from -0.0625 to 0.0625
- page_pool: bfloat16 [32, 512, 2048], P('req', 'grp'), may hold values from -68 to 68
- stretch_ids: int32 [4, 4], replicated, may hold values from 0 to 31, as said below
- page_slot: int32 [32], replicated, may hold values from 0 to 31, as said below
- picked: int32 [4, 4, 24], replicated, may hold values from 0 to 511, as said below
- question_len: int32 [4], replicated, may hold values from 1 to 64
Outputs:
- attn_out: bfloat16 [4, 160, 8192], P('req', None, 'grp')
- joined_pool: bfloat16 [32, 512, 2048], P('req', 'grp')
The draws below stay inside these ranges and needn't reach their ends.
Inputs may be any that keep to these rules, and one draw needn't show every extreme that they name: page_slot is a permutation. All ids in stretch_ids are distinct; of each request's 4 passages, exactly 1 has page_slot // 8 equal to each holder index. `picked`: the 24 positions of one passage are distinct.
All inputs are finite; a program needn't handle non-finite values.
Results may differ from the reference program's by a relative error of at most 0.0065.
The reference program's roundings to bfloat16 on the way (of `normed`, `keys` and `attention`) count: a program that leaves them out, or rounds other values in their place, can miss the bound.
Values may be sent and summed in bfloat16 or wider, within the bound.
A program may use at most 64 MiB of HBM per device.

```python
import jax
import jax.numpy as jnp
from jax import lax

D = 8192
HQ = 64
KVH = 8
HD = 128
SPAN_TOK = 512
RCH = 24
QMAX = 64
PER_HOLDER = 1
SPANS = 4
POOL_REQ = 8
POOL = 32
ROWS = 160
KVW = 2048
N_REQ = 4


def draw_page_pool(key, part):
    key = jax.random.fold_in(key, 11)
    first = jax.random.fold_in(key, 0)
    shape = (POOL, SPAN_TOK, 2 * KVH * HD)
    values = jnp.clip(jax.random.normal(first, shape, jnp.float32), -6.0, 6.0)
    return values.astype(jnp.bfloat16)


def draw_page_slot(key, part):
    shared = jax.random.permutation(key, POOL).astype(jnp.int32)
    return shared


def draw_stretch_ids(key, part):
    shared = jax.random.permutation(key, POOL).astype(jnp.int32)
    key = jax.random.fold_in(key, 12)
    first, second = jax.random.split(key)
    holder_keys = jax.random.split(first, N_REQ)
    local_perm = jax.vmap(lambda sub: jax.random.permutation(sub, POOL_REQ))(holder_keys)
    chosen = local_perm[:, :SPANS].reshape(N_REQ, N_REQ, PER_HOLDER)
    base = (jnp.arange(N_REQ, dtype=jnp.int32) * POOL_REQ)[:, None, None]
    positions = jnp.transpose(chosen + base, (1, 0, 2)).reshape(N_REQ, SPANS)
    order_keys = jax.random.split(second, N_REQ)
    orders = jax.vmap(lambda sub: jax.random.permutation(sub, SPANS))(order_keys)
    positions = jnp.take_along_axis(positions, orders, axis=1)
    inverse = jnp.zeros((POOL,), jnp.int32).at[shared].set(jnp.arange(POOL, dtype=jnp.int32))
    return inverse[positions].astype(jnp.int32)


def draw_picked(key, part):
    key = jax.random.fold_in(key, 13)
    keys = jax.random.split(key, N_REQ * SPANS)
    chosen = jax.vmap(lambda sub: jax.random.permutation(sub, SPAN_TOK)[:RCH])(keys)
    return chosen.reshape(N_REQ, SPANS, RCH).astype(jnp.int32)


def plant(array, key, least, largest):
    dims = array.shape
    spot = [jax.random.randint(jax.random.fold_in(key, axis), (), 0, dims[axis]) for axis in range(len(dims))]
    array = array.at[tuple(spot)].set(least)
    longest = dims.index(max(dims))
    spot[longest] = (spot[longest] + 1) % dims[longest]
    return array.at[tuple(spot)].set(largest)


def block_levels(own_key, dims, shards, smallest, top_value):
    factor_of = 1.0
    for axis_at, parts in shards:
        heights = jax.random.uniform(jax.random.fold_in(jax.random.fold_in(own_key, 6), axis_at), (parts,), jnp.float32, smallest / len(shards), top_value / len(shards))
        factor_of = factor_of * jnp.repeat(jnp.exp(heights), dims[axis_at] // parts).reshape((-1,) + (1,) * (len(dims) - 1 - axis_at))
    return factor_of


def centred(own_key, shape, scale, limit, cuts=(), kind=jnp.bfloat16):
    result = jax.random.normal(own_key, shape, jnp.float32) * scale
    if len(cuts) > 0:
        result = block_levels(own_key, shape, cuts, -0.22, 0.18) * result
    return jnp.clip(result, min=-limit, max=limit).astype(kind)


def setup_inputs(seed: int = 0) -> dict:
    arg_keys = jax.random.split(jax.random.key(seed), 11)
    rows_in = centred(arg_keys[0], (N_REQ, ROWS, D), 1.0, 6.0, ((0, 4),))
    norm_gain = jnp.clip(1.0 + 0.1 * jax.random.normal(arg_keys[1], (D,), jnp.float32), 0.5, 1.5)
    w_query = centred(arg_keys[2], (D, HQ * HD), D ** -0.5, 0.0625, ((1, 32),))
    w_keyval = centred(arg_keys[3], (D, KVW), D ** -0.5, 0.0625, ((1, 32),))
    w_out = centred(arg_keys[4], (HQ * HD, D), (HQ * HD) ** -0.5, 0.0625, ((1, 32),))
    page_pool = draw_page_pool(jax.random.fold_in(arg_keys[10], 71), 0)
    stretch_ids = draw_stretch_ids(jax.random.fold_in(arg_keys[10], 71), 0)
    page_slot = draw_page_slot(jax.random.fold_in(arg_keys[10], 71), 0)
    picked = draw_picked(jax.random.fold_in(arg_keys[10], 71), 0)
    question_len = plant(jax.random.randint(arg_keys[9], (N_REQ,), 1, QMAX + 1), jax.random.fold_in(arg_keys[9], 1), 1, QMAX).astype(jnp.int32)
    return dict(rows_in=rows_in, norm_gain=norm_gain, w_query=w_query, w_keyval=w_keyval, w_out=w_out, page_pool=page_pool, stretch_ids=stretch_ids, page_slot=page_slot, picked=picked, question_len=question_len)


EPS = 1e-05

def reference(rows_in, norm_gain, w_query, w_keyval, w_out, page_pool, stretch_ids, page_slot, picked, question_len):
    group = HQ // KVH
    context = SPANS * SPAN_TOK
    leading = SPANS * RCH
    scale = 1.0 / float(HD) ** 0.5
    pool = page_pool
    results = []
    for request in range(N_REQ):
        inputs = rows_in[request].astype(jnp.float32)
        normed = (inputs * lax.rsqrt(lax.optimization_barrier(jnp.mean(inputs * inputs, axis=-1, keepdims=True)) + EPS) * norm_gain).astype(jnp.bfloat16)
        query = jnp.dot(normed, w_query, preferred_element_type=jnp.float32).astype(jnp.bfloat16)
        fresh = jnp.dot(normed, w_keyval, preferred_element_type=jnp.float32).astype(jnp.bfloat16)
        where_at = page_slot[stretch_ids[request]].astype(jnp.int32)
        pages = pool[where_at]
        chosen = picked[request].astype(jnp.int32)
        span_rows = jnp.arange(SPANS, dtype=jnp.int32)[:, None]
        pages = pages.at[span_rows, chosen].set(fresh[:leading].reshape(SPANS, RCH, 2 * KVH * HD))
        pool = pool.at[where_at].set(pages)
        keys = jnp.concatenate([pages.reshape(context, 2 * KVH * HD), fresh[leading:]], axis=0)
        key_pos = jnp.arange(context + QMAX, dtype=jnp.int32)
        key_live = key_pos < context + question_len[request]
        query_pos = jnp.concatenate([(span_rows * SPAN_TOK + chosen).reshape(-1), context + jnp.arange(QMAX, dtype=jnp.int32)])
        visible = (key_pos[None, :] <= query_pos[:, None]) & key_live[None, :]
        key_data = keys[:, :KVH * HD].astype(jnp.float32).reshape(-1, KVH, HD)
        val_data = keys[:, KVH * HD:].astype(jnp.float32).reshape(-1, KVH, HD)
        query_data = query.astype(jnp.float32).reshape(ROWS, HQ, HD)

        def one_head(head):
            query_head = jnp.take(query_data, head, axis=1)
            key_head = jnp.take(key_data, head // group, axis=1)
            val_head = jnp.take(val_data, head // group, axis=1)
            scores = jnp.dot(query_head, key_head.T, precision=lax.Precision.HIGHEST) * scale
            scores = jnp.where(visible, scores, -1e+30)
            peak = lax.optimization_barrier(jnp.max(scores, axis=-1, keepdims=True))
            weights = jnp.where(visible, jnp.exp(scores - peak), 0.0)
            total = lax.optimization_barrier(jnp.sum(weights, axis=-1, keepdims=True))
            return jnp.dot(weights, val_head, precision=lax.Precision.HIGHEST) / total
        heads_out = lax.map(one_head, jnp.arange(HQ, dtype=jnp.int32))
        attention = jnp.transpose(heads_out, (1, 0, 2)).reshape(ROWS, HQ * HD).astype(jnp.bfloat16)
        projected = jnp.dot(attention, w_out, preferred_element_type=jnp.float32)
        valid = jnp.concatenate([jnp.ones((leading,), dtype=bool), jnp.arange(QMAX, dtype=jnp.int32) < question_len[request]])
        results.append(jnp.where(valid[:, None], projected, 0.0).astype(jnp.bfloat16))
    return (jnp.stack(results), pool)
```

```python
import functools

import jax
import jax.numpy as jnp
from jax import lax
from jax.experimental import pallas as pl
from jax.experimental.pallas import tpu as pltpu
from jax.sharding import PartitionSpec as P

MESH = pl.DeviceIdType.MESH
F32 = jnp.float32
BF16 = jnp.bfloat16
HD = 128
KVH = 8
ROWS = 160
RCH = 24
SPANS = 4
D = 8192
KEYS = 2048
EPS = 1e-05
SCALE = 1.0 / float(HD) ** 0.5
NEG = -1e30
FAR = 1e9
LINE = (0, 1, 3, 2)


def nt_dot(a, b):
    return lax.dot_general(a, b, (((1,), (1,)), ((), ())), preferred_element_type=F32)


def nn_dot(a, b):
    return jnp.dot(a, b, preferred_element_type=F32)


def by_index(index, values):
    low = jnp.where(index == 0, values[0], values[1])
    return jnp.where(index < 2, low, jnp.where(index == 2, values[2], values[3]))


def to_column(row):
    n = row.shape[1]
    eye = lax.broadcasted_iota(jnp.int32, (n, n), 0) == lax.broadcasted_iota(jnp.int32, (n, n), 1)
    return jnp.sum(jnp.where(eye, jnp.broadcast_to(row, (n, n)), 0.0), axis=1, keepdims=True)


def kernel(
    rows_hbm,
    gain_hbm,
    wq_hbm,
    wk_hbm,
    wo_hbm,
    pool_hbm,
    ids,
    slots,
    picked,
    qlen,
    out_ref,
    joined_hbm,
    rows_v,
    gain_v,
    nrm,
    wq_v,
    wk_v,
    wo_v,
    pool_v,
    joined_v,
    sx,
    rx,
    kv,
    kvp,
    fr,
    fk,
    q2,
    scores,
    peak,
    total,
    part,
    gath,
    acc,
    sj,
    rj1,
    rj,
    ld,
    xs_s,
    xs_r,
    zs_s,
    zs_r,
    cs_s,
    cs_r,
    fr_s,
    fr_r,
    js_s,
    js_r,
    jz_s,
    jz_r,
    g_s,
    g_r,
    gc_s,
    gc_r,
    out_sem,
):
    r = lax.axis_index("req")
    m = lax.axis_index("grp")
    z = lax.div(m, 8)
    y = lax.rem(lax.div(m, 2), 4)
    c = lax.rem(m, 2)
    chip = lax.div(m, 2)
    k = lax.div(m, 4)
    sib = (r, m + 1 - 2 * c)

    def load(src, dst, i):
        cp = pltpu.make_async_copy(src, dst, ld.at[i])
        cp.start()
        return cp

    def push(src, dst, send, recv, dev):
        pltpu.make_async_remote_copy(
            src_ref=src, dst_ref=dst, send_sem=send, recv_sem=recv, device_id=dev, device_id_type=MESH
        ).start()

    def wait_all(ref, sem):
        pltpu.make_async_copy(ref, ref, sem).wait()

    ld_pool = load(pool_hbm, pool_v, 0)
    ld_rows = [
        load(rows_hbm.at[0, pl.ds(32 * i, 32)], rows_v.at[pl.ds(32 * i, 32)], 1 + i) for i in range(5)
    ]
    ld_gain = load(gain_hbm, gain_v, 6)
    ld_wk = load(wk_hbm, wk_v.at[pl.ds(pl.multiple_of(64 * c, 64), 64)], 7)
    ld_wq = [
        load(wq_hbm.at[pl.ds(2048 * i, 2048)], wq_v.at[pl.ds(2048 * i, 2048)], 8 + i) for i in range(4)
    ]
    ld_wo = load(wo_hbm, wo_v, 12)

    barrier = pltpu.get_barrier_semaphore()

    def greet(d, carry):
        pl.semaphore_signal(barrier, inc=1, device_id=(r, lax.rem(m + d, 32)), device_id_type=MESH)
        return carry

    lax.fori_loop(1, 32, greet, 0)
    for d in range(1, 4):
        pl.semaphore_signal(barrier, inc=1, device_id=(lax.rem(r + d, 4), m), device_id_type=MESH)

    wk_v[pl.ds(pl.multiple_of(64 - 64 * c, 64), 64), :] = jnp.zeros((64, D), BF16)

    place = [[slots[ids[q, s]] for s in range(SPANS)] for q in range(4)]
    send_slot, send_span = [], []
    for q in range(4):
        slot_q, span_q = 0, 0
        for s in range(SPANS):
            here = (place[q][s] >> 3) == r
            slot_q = slot_q + jnp.where(here, place[q][s] & 7, 0)
            span_q = span_q + jnp.where(here, s, 0)
        send_slot.append(slot_q)
        send_span.append(span_q)
    own_place = [slots[ids[r, s]] for s in range(SPANS)]
    span_of = []
    for x in range(4):
        span_x = 0
        for s in range(SPANS):
            span_x = span_x + jnp.where((own_place[s] >> 3) == x, s, 0)
        span_of.append(span_x)

    ld_pool.wait()
    row = lax.broadcasted_iota(jnp.int32, (64, 128), 0)
    wanted = by_index(row >> 4, send_slot) * 16 + (row & 15)
    pick_page = jnp.where(lax.broadcasted_iota(jnp.int32, (64, 128), 1) == wanted, 1.0, 0.0).astype(BF16)
    for h in range(2 * KVH):
        piece = nn_dot(pick_page, pool_v[:, :, h * HD : (h + 1) * HD].reshape(128, HD)).astype(BF16)
        for q in range(4):
            sx[q, h % KVH, h // KVH] = piece[16 * q : 16 * (q + 1)]
    pl.semaphore_wait(barrier, 34)
    for d in (1, 3, 2):
        q = lax.rem(r + d, 4)
        push(sx.at[q], rx.at[r], xs_s.at[0], xs_r.at[d - 1], (q, m))

    def spread(src, x):
        def one(d, carry):
            t = lax.rem(chip + d, 16)
            push(
                src.at[lax.div(t, 2)],
                kv.at[c, chip, x],
                zs_s.at[0],
                zs_r.at[z],
                (r, 2 * t + c),
            )
            return carry

        pltpu.make_async_copy(src.at[k], kv.at[c, chip, x], zs_r.at[z]).start()
        lax.fori_loop(1, 16, one, 0)

    spread(sx.at[r], r)

    ld_gain.wait()
    for i in range(5):
        ld_rows[i].wait()

    def norm(i, carry):
        at = pl.ds(pl.multiple_of(32 * i, 32), 32)
        squares = jnp.zeros((32, 128), F32)
        for j in range(D // 128):
            v = rows_v[at, j * 128 : (j + 1) * 128].astype(F32)
            squares = squares + v * v
        mean = jnp.sum(squares, axis=1, keepdims=True) * (1.0 / D)
        inv = jnp.broadcast_to(lax.rsqrt(mean + EPS), (32, 128))
        for j in range(D // 128):
            v = rows_v[at, j * 128 : (j + 1) * 128].astype(F32)
            nrm[at, j * 128 : (j + 1) * 128] = (v * inv * gain_v[:, j * 128 : (j + 1) * 128]).astype(BF16)
        return carry

    lax.fori_loop(0, 5, norm, 0)

    ld_wk.wait()
    part[0:ROWS, :] = jnp.zeros((ROWS, HD), F32)

    def kv_step(i, carry):
        cols = pl.ds(pl.multiple_of(1024 * i, 1024), 1024)
        part[0:ROWS, :] += nt_dot(nrm[:, cols], wk_v[:, cols])
        return carry

    lax.fori_loop(0, 8, kv_step, 0)
    kvp[...] = part[0:ROWS, :].astype(BF16)
    head_to = lax.div(lax.rem(m, 16), 2)
    fr_slot = lax.div(m, 16) * 2 + c
    for i in range(4):
        t = 4 * head_to + i

        @pl.when(t == m)
        def _():
            pltpu.make_async_copy(kvp, fr.at[fr_slot], fr_r.at[0]).start()

        @pl.when(t != m)
        def _():
            push(kvp, fr.at[fr_slot], fr_s.at[0], fr_r.at[0], (r, t))

    for d in (1, 3, 2):
        x = lax.rem(r + 4 - d, 4)
        wait_all(rx.at[x], xs_r.at[d - 1])
        spread(rx.at[x], x)

    acc[...] = jnp.zeros((ROWS, 2 * HD), F32)
    for i in range(4):
        ld_wq[i].wait()

        def q_step(j, carry):
            at = pl.multiple_of(2048 * i + 1024 * j, 1024)
            acc[...] += nn_dot(nrm[:, pl.ds(at, 1024)], wq_v[pl.ds(at, 1024), :])
            return carry

        lax.fori_loop(0, 2, q_step, 0)
    q2[0:ROWS, :] = acc[:, 0:HD].astype(BF16)
    q2[ROWS : 2 * ROWS, :] = acc[:, HD : 2 * HD].astype(BF16)

    own_picked = picked[r].astype(F32)
    cols = [to_column(own_picked[s : s + 1, :]) + 512.0 * s for s in range(SPANS)]
    question = lax.broadcasted_iota(jnp.int32, (64, 1), 0).astype(F32)
    own_len = qlen[r].astype(F32)
    row_pos = jnp.concatenate(cols + [question + float(KEYS)], axis=0)
    key_col = jnp.concatenate(cols + [jnp.where(question < own_len, question + float(KEYS), FAR)], axis=0)
    eye = lax.broadcasted_iota(jnp.int32, (ROWS, 256), 0) == lax.broadcasted_iota(jnp.int32, (ROWS, 256), 1)
    fresh_pos = jnp.sum(jnp.where(eye, jnp.broadcast_to(key_col, (ROWS, 256)), 0.0), axis=0, keepdims=True)
    fresh_pos = jnp.where(lax.broadcasted_iota(jnp.int32, (1, 256), 1) < ROWS, fresh_pos, FAR)
    row_pos_b = jnp.broadcast_to(row_pos, (ROWS, 256))
    picked_b = row_pos_b[0 : SPANS * RCH]

    wait_all(fr, fr_r.at[0])
    row = lax.broadcasted_iota(jnp.int32, (SPANS * RCH, 256), 0)
    wanted = by_index(lax.div(row, RCH), span_of) * RCH + lax.rem(row, RCH)
    pick_rows = jnp.where(lax.broadcasted_iota(jnp.int32, (SPANS * RCH, 256), 1) == wanted, 1.0, 0.0).astype(BF16)
    by_holder = []
    for s in range(2):
        fk[s, 0:ROWS, :] = (fr[2 * s].astype(F32) + fr[2 * s + 1].astype(F32)).astype(BF16)
        fk[s, ROWS:256, :] = jnp.zeros((256 - ROWS, HD), BF16)
        by_holder.append(nn_dot(pick_rows, fk[s]))
    for x in range(4):
        sj[x] = jnp.concatenate([b[x * RCH : (x + 1) * RCH] for b in by_holder], axis=0).astype(BF16)
    for d in (1, 3, 2):
        x = lax.rem(r + d, 4)
        push(sj.at[x], rj1.at[r], js_s.at[0], js_r.at[d - 1], (x, m))
    rj1[r] = sj[r]

    def score(at, keys, key_pos):
        s = nt_dot(q2[...], keys) * SCALE
        seen = row_pos_b >= jnp.broadcast_to(key_pos, (ROWS, 256))
        for half in range(2):
            rows = slice(half * ROWS, (half + 1) * ROWS)
            masked = jnp.where(seen, s[rows], NEG)
            scores[at, rows, :] = masked
            peak[rows, :] = jnp.maximum(peak[rows, :], jnp.maximum(masked[:, :128], masked[:, 128:]))

    peak[...] = jnp.full((2 * ROWS, 128), NEG, F32)
    score(8, fk[0], fresh_pos)

    lane = lax.broadcasted_iota(jnp.int32, (1, 256), 1)
    lane_x = (lane >> 4) & 3
    span_lane = by_index(lane_x, span_of)
    lane_pos = span_lane * 512 + (lane >> 6) * 32 + (lane & 15)

    def page_keys(cc, zz):
        pos = (lane_pos + (zz * 128 + cc * 16)).astype(F32)
        same = picked_b == jnp.broadcast_to(pos, (SPANS * RCH, 256))
        gone = jnp.max(jnp.where(same, 1.0, 0.0), axis=0, keepdims=True)
        return jnp.where(gone > 0.5, FAR, pos)

    for d in (0, 1, 3, 2):
        zz = lax.rem(z + d, 4)
        group = kv.at[c, pl.ds(4 * zz, 4)]
        wait_all(group, zs_r.at[zz])
        push(group, group, cs_s.at[0], cs_r.at[zz], sib)

    def own_scores(zz, carry):
        keys = kv[c, pl.ds(4 * zz, 4), :, 0].reshape(256, HD)
        score(zz, keys, page_keys(c, zz))
        return carry

    lax.fori_loop(0, 4, own_scores, 0)

    for d in (1, 3, 2):
        x = lax.rem(r + 4 - d, 4)
        wait_all(rj1.at[x], js_r.at[d - 1])
    rj[k] = rj1[...]

    def spread_fresh(d, carry):
        t = lax.rem(k + d, 8)
        push(rj1, rj.at[k], jz_s.at[0], jz_r.at[0], (r, (2 * t + lax.rem(y, 2)) * 2 + c))
        return carry

    lax.fori_loop(1, 8, spread_fresh, 0)

    def sib_scores(zz, carry):
        wait_all(kv.at[1 - c, pl.ds(4 * zz, 4)], cs_r.at[zz])
        keys = kv[1 - c, pl.ds(4 * zz, 4), :, 0].reshape(256, HD)
        score(4 + zz, keys, page_keys(1 - c, zz))
        return carry

    lax.fori_loop(0, 4, sib_scores, 0)

    peak[...] = jnp.broadcast_to(jnp.max(peak[...], axis=1, keepdims=True), (2 * ROWS, 128))
    total[...] = jnp.zeros((2 * ROWS, 128), F32)
    part[...] = jnp.zeros((2 * ROWS, HD), F32)

    def weigh(at, vals):
        top = peak[...]
        w0 = jnp.exp(scores[at, :, 0:128] - top)
        w1 = jnp.exp(scores[at, :, 128:256] - top)
        total[...] += w0 + w1
        part[...] += nn_dot(jnp.concatenate([w0, w1], axis=1).astype(BF16), vals)

    def page_values(i, carry):
        far = lax.div(i, 4)
        cc = c + far * (1 - 2 * c)
        zz = lax.rem(i, 4)
        weigh(i, kv[cc, pl.ds(4 * zz, 4), :, 1].reshape(256, HD))
        return carry

    lax.fori_loop(0, 8, page_values, 0)
    weigh(8, fk[1])
    att = part[...] / jnp.sum(total[...], axis=1, keepdims=True)
    gath[c, chip, :, 0:HD] = att[0:ROWS].astype(BF16)
    gath[c, chip, :, HD : 2 * HD] = att[ROWS : 2 * ROWS].astype(BF16)

    def chip_at(cc, df, ds):
        f = lax.rem(y * (1 - cc) + z * cc + df, 4)
        s = lax.rem(z * (1 - cc) + y * cc + ds, 4)
        return (4 * s + f) * (1 - cc) + (4 * f + s) * cc

    def forward(block, df, ds):
        ref = gath.at[c, block]
        push(ref, ref, g_s.at[0], g_r.at[block], (r, 2 * chip_at(c, df, ds) + c))

    def across(block):
        ref = gath.at[c, block]
        push(ref, ref, gc_s.at[0], gc_r.at[block], sib)

    def arrived(block):
        wait_all(gath.at[c, block], g_r.at[block])

    def project(cc, ds, wait):
        def one(df, carry):
            block = chip_at(cc, df, ds)
            if wait:
                wait_all(gath.at[cc, block], gc_r.at[block])
            at = pl.multiple_of((2 * block + cc) * 256, 256)
            acc[...] += nn_dot(gath[cc, block], wo_v[pl.ds(at, 256), :])
            return carry

        lax.fori_loop(0, 4, one, 0)

    for df, ds in ((1, 0), (3, 0), (2, 0), (0, 1), (0, 3)):
        forward(chip, df, ds)
    across(chip)
    acc[...] = jnp.zeros((ROWS, 2 * HD), F32)
    for df in (1, 3, 2):
        block = chip_at(c, df, 0)
        arrived(block)
        forward(block, 0, 1)
        forward(block, 0, 3)
        across(block)
    ld_wo.wait()
    project(c, 0, False)
    for df in LINE:
        for ds in (1, 3):
            block = chip_at(c, df, ds)
            arrived(block)
            if (ds == 3) == (df in (0, 2)):
                forward(block, 0, 4 - ds)
            across(block)
    project(1 - c, 0, True)
    project(c, 1, False)
    project(c, 3, False)

    wait_all(rj.at[pl.ds(0, 7)], jz_r.at[0])
    col = lax.broadcasted_iota(jnp.int32, (RCH, 192), 1)
    col_req = lax.div(col, 48)
    col_in = lax.rem(col, 48)
    row_in = lax.broadcasted_iota(jnp.int32, (RCH, 192), 0)
    target = jnp.zeros((1, 192), F32)
    low = (m * 16).astype(F32)
    for q in range(4):
        pq = picked[q].astype(F32)
        mine = jnp.zeros((1, RCH), F32)
        for s in range(SPANS):
            mine = mine + jnp.where(send_span[q] == s, pq[s : s + 1, :], 0.0)
        mine = mine - low
        mine = jnp.where((mine >= 0.0) & (mine < 16.0), mine + (send_slot[q] * 16).astype(F32), -1.0)
        fits = (col_req == q) & ((col_in == row_in) | (col_in == row_in + RCH))
        target = target + jnp.sum(
            jnp.where(fits, jnp.broadcast_to(to_column(mine), (RCH, 192)), 0.0), axis=0, keepdims=True
        )
    line = lax.broadcasted_iota(jnp.int32, (128, 192), 0).astype(F32)
    is_key = lax.rem(lax.broadcasted_iota(jnp.int32, (128, 192), 1), 48) < RCH
    match = line == jnp.broadcast_to(target, (128, 192))
    pick_key = jnp.where(match & is_key, 1.0, 0.0)
    pick_val = jnp.where(match & jnp.logical_not(is_key), 1.0, 0.0)
    hit = jnp.broadcast_to(jnp.max(pick_key, axis=1, keepdims=True), (128, HD)) > 0.5
    pick = jnp.concatenate([pick_key, pick_val], axis=0).astype(BF16)
    for h in range(KVH):
        new = nn_dot(pick, rj[h].reshape(192, HD))
        for s in range(2):
            at = slice(1024 * s + h * HD, 1024 * s + (h + 1) * HD)
            old = pool_v[:, :, at].astype(F32).reshape(128, HD)
            joined_v[:, :, at] = (
                jnp.where(hit, new[128 * s : 128 * (s + 1)], old).astype(BF16).reshape(8, 16, HD)
            )
    joined_out = pltpu.make_async_copy(joined_v, joined_hbm, out_sem.at[0])
    joined_out.start()

    project(1 - c, 1, True)
    project(1 - c, 3, True)
    for df in LINE:
        block = chip_at(c, df, 2)
        arrived(block)
        across(block)
    project(c, 2, False)
    project(1 - c, 2, True)
    live = lax.broadcasted_iota(jnp.int32, (ROWS, 2 * HD), 0) < SPANS * RCH + qlen[r]
    out_ref[0] = jnp.where(live, acc[...], 0.0).astype(BF16)

    joined_out.wait()
    wait_all(rx.at[pl.ds(0, 3)], xs_s.at[0])
    wait_all(kv.at[0, pl.ds(0, 15)], zs_s.at[0])
    wait_all(kv.at[0], cs_s.at[0])

    @pl.when(head_to == k)
    def _():
        wait_all(fr.at[pl.ds(0, 3)], fr_s.at[0])

    @pl.when(head_to != k)
    def _():
        wait_all(fr, fr_s.at[0])

    wait_all(rj1.at[pl.ds(0, 3)], js_s.at[0])
    wait_all(rj.at[pl.ds(0, 7)], jz_s.at[0])
    wait_all(gath.at[0, pl.ds(0, 15)], g_s.at[0])
    wait_all(gath.at[0], gc_s.at[0])


def local(
    rows_in, norm_gain, w_query, w_keyval, w_out, page_pool, stretch_ids, page_slot, picked, question_len
):
    any_spec = pl.BlockSpec(memory_space=pl.ANY)
    smem = pl.BlockSpec(memory_space=pltpu.SMEM)
    vmem = pl.BlockSpec(memory_space=pltpu.VMEM)
    sem = pltpu.SemaphoreType.DMA
    return pl.pallas_call(
        kernel,
        out_shape=(
            jax.ShapeDtypeStruct((1, ROWS, 2 * HD), BF16),
            jax.ShapeDtypeStruct(page_pool.shape, BF16),
        ),
        in_specs=[any_spec] * 6 + [smem, smem, vmem, smem],
        out_specs=(vmem, any_spec),
        scratch_shapes=[
            pltpu.VMEM((ROWS, D), BF16),
            pltpu.VMEM((1, D), F32),
            pltpu.VMEM((ROWS, D), BF16),
            pltpu.VMEM((D, 2 * HD), BF16),
            pltpu.VMEM((HD, D), BF16),
            pltpu.VMEM((D, 2 * HD), BF16),
            pltpu.VMEM((8, 16, 2048), BF16),
            pltpu.VMEM((8, 16, 2048), BF16),
            pltpu.VMEM((4, KVH, 2, 16, HD), BF16),
            pltpu.VMEM((4, KVH, 2, 16, HD), BF16),
            pltpu.VMEM((2, 16, 4, 2, 16, HD), BF16),
            pltpu.VMEM((ROWS, HD), BF16),
            pltpu.VMEM((4, ROWS, HD), BF16),
            pltpu.VMEM((2, 256, HD), BF16),
            pltpu.VMEM((2 * ROWS, HD), BF16),
            pltpu.VMEM((9, 2 * ROWS, 256), F32),
            pltpu.VMEM((2 * ROWS, 128), F32),
            pltpu.VMEM((2 * ROWS, 128), F32),
            pltpu.VMEM((2 * ROWS, HD), F32),
            pltpu.VMEM((2, 16, ROWS, 2 * HD), BF16),
            pltpu.VMEM((ROWS, 2 * HD), F32),
            pltpu.VMEM((4, 2 * RCH, HD), BF16),
            pltpu.VMEM((4, 2 * RCH, HD), BF16),
            pltpu.VMEM((KVH, 4, 2 * RCH, HD), BF16),
            sem((13,)),
            sem((1,)),
            sem((3,)),
            sem((1,)),
            sem((4,)),
            sem((1,)),
            sem((4,)),
            sem((1,)),
            sem((1,)),
            sem((1,)),
            sem((3,)),
            sem((1,)),
            sem((1,)),
            sem((1,)),
            sem((16,)),
            sem((1,)),
            sem((16,)),
            sem((1,)),
        ],
        compiler_params=pltpu.CompilerParams(
            collective_id=0, has_side_effects=True, vmem_limit_bytes=56 * 1024 * 1024
        ),
        name="joined_attention",
    )(
        rows_in,
        norm_gain.reshape(1, D),
        w_query,
        w_keyval.T,
        w_out,
        page_pool,
        stretch_ids,
        page_slot,
        picked,
        question_len,
    )


def solution(mesh):
    in_specs = (
        P("req", None, None),
        P(),
        P(None, "grp"),
        P(None, "grp"),
        P(None, "grp"),
        P("req", "grp", None),
        P(),
        P(),
        P(),
        P(),
    )
    out_specs = (P("req", None, "grp"), P("req", "grp", None))
    return jax.shard_map(local, mesh=mesh, in_specs=in_specs, out_specs=out_specs, check_vma=False)
```

```python
import functools

import jax
import jax.numpy as jnp
from jax import lax
from jax.experimental import pallas as pl
from jax.experimental.pallas import tpu as pltpu
from jax.sharding import PartitionSpec as P

MESH = pl.DeviceIdType.MESH
F32 = jnp.float32
BF16 = jnp.bfloat16
HD = 128
KVH = 8
ROWS = 160
RCH = 24
SPANS = 4
D = 8192
KEYS = 2048
EPS = 1e-05
SCALE = 1.0 / float(HD) ** 0.5
NEG = -1e30
FAR = 1e9
LINE = (0, 1, 3, 2)
HOPS = (0, 1, 2, 1)
FARTHEST_FIRST = sorted(
    [(n // 16, n // 4 % 4, n % 4) for n in range(1, 64)], key=lambda steps: -sum(HOPS[d] for d in steps)
)


def nt_dot(a, b):
    return lax.dot_general(a, b, (((1,), (1,)), ((), ())), preferred_element_type=F32)


def nn_dot(a, b):
    return jnp.dot(a, b, preferred_element_type=F32)


def by_index(index, values):
    low = jnp.where(index == 0, values[0], values[1])
    return jnp.where(index < 2, low, jnp.where(index == 2, values[2], values[3]))


def to_column(row):
    n = row.shape[1]
    eye = lax.broadcasted_iota(jnp.int32, (n, n), 0) == lax.broadcasted_iota(jnp.int32, (n, n), 1)
    return jnp.sum(jnp.where(eye, jnp.broadcast_to(row, (n, n)), 0.0), axis=1, keepdims=True)


def kernel(
    rows_hbm,
    gain_hbm,
    wq_hbm,
    wk_hbm,
    wo_hbm,
    pool_hbm,
    ids,
    slots,
    picked,
    qlen,
    out_ref,
    joined_v,
    rows_v,
    gain_v,
    nrm,
    wq_v,
    wk_v,
    wo_v,
    pool_v,
    sx,
    kv,
    kvp,
    fr,
    fk,
    q2,
    scores,
    peak,
    total,
    part,
    gath,
    acc,
    sj,
    rj1,
    rj,
    ld,
    zs_s,
    zs_r,
    cs_s,
    cs_r,
    fr_s,
    fr_r,
    js_s,
    js_r,
    jz_s,
    jz_r,
    g_s,
    g_r,
    gc_s,
    gc_r,
):
    r = lax.axis_index("req")
    m = lax.axis_index("grp")
    z = lax.div(m, 8)
    y = lax.rem(lax.div(m, 2), 4)
    c = lax.rem(m, 2)
    chip = lax.div(m, 2)
    k = lax.div(m, 4)
    sib = (r, m + 1 - 2 * c)

    def load(src, dst, i):
        cp = pltpu.make_async_copy(src, dst, ld.at[i])
        cp.start()
        return cp

    def push(src, dst, send, recv, dev):
        pltpu.make_async_remote_copy(
            src_ref=src, dst_ref=dst, send_sem=send, recv_sem=recv, device_id=dev, device_id_type=MESH
        ).start()

    def wait_all(ref, sem):
        pltpu.make_async_copy(ref, ref, sem).wait()

    barrier = pltpu.get_barrier_semaphore()

    def others(act, first=0, last=63):
        for dx, dy, dz in FARTHEST_FIRST[first:last]:
            act(lax.rem(r + dx, 4), 4 * lax.rem(z + dz, 4) + lax.rem(y + dy, 4))

    def greet(q, t):
        pl.semaphore_signal(barrier, inc=1, device_id=(q, 2 * t + c), device_id_type=MESH)

    others(greet)
    pl.semaphore_signal(barrier, inc=1, device_id=sib, device_id_type=MESH)

    ld_pool = load(pool_hbm, pool_v, 0)
    ld_rows = [
        load(rows_hbm.at[0, pl.ds(32 * i, 32)], rows_v.at[pl.ds(32 * i, 32)], 1 + i) for i in range(5)
    ]
    ld_gain = load(gain_hbm, gain_v, 6)
    ld_wk = load(wk_hbm, wk_v.at[pl.ds(pl.multiple_of(64 * c, 64), 64)], 7)

    wk_v[pl.ds(pl.multiple_of(64 - 64 * c, 64), 64), :] = jnp.zeros((64, D), BF16)

    place = [[slots[ids[q, s]] for s in range(SPANS)] for q in range(4)]
    send_slot, send_span = [], []
    for q in range(4):
        slot_q, span_q = 0, 0
        for s in range(SPANS):
            here = (place[q][s] >> 3) == r
            slot_q = slot_q + jnp.where(here, place[q][s] & 7, 0)
            span_q = span_q + jnp.where(here, s, 0)
        send_slot.append(slot_q)
        send_span.append(span_q)
    own_place = [slots[ids[r, s]] for s in range(SPANS)]
    span_of = []
    for x in range(4):
        span_x = 0
        for s in range(SPANS):
            span_x = span_x + jnp.where((own_place[s] >> 3) == x, s, 0)
        span_of.append(span_x)

    ld_pool.wait()
    row = lax.broadcasted_iota(jnp.int32, (64, 128), 0)
    wanted = by_index(row >> 4, send_slot) * 16 + (row & 15)
    pick_page = jnp.where(lax.broadcasted_iota(jnp.int32, (64, 128), 1) == wanted, 1.0, 0.0).astype(BF16)
    for h in range(2 * KVH):
        piece = nn_dot(pick_page, pool_v[:, :, h * HD : (h + 1) * HD].reshape(128, HD)).astype(BF16)
        for q in range(4):
            sx[q, h % KVH, h // KVH] = piece[16 * q : 16 * (q + 1)]
    ld_gain.wait()
    for i in range(5):
        ld_rows[i].wait()

    ld_wq = [
        load(wq_hbm.at[pl.ds(2048 * i, 2048)], wq_v.at[pl.ds(2048 * i, 2048)], 8 + i) for i in range(4)
    ]

    def norm(i, carry):
        at = pl.ds(pl.multiple_of(32 * i, 32), 32)
        squares = jnp.zeros((32, 128), F32)
        for j in range(D // 128):
            v = rows_v[at, j * 128 : (j + 1) * 128].astype(F32)
            squares = squares + v * v
        mean = jnp.sum(squares, axis=1, keepdims=True) * (1.0 / D)
        inv = jnp.broadcast_to(lax.rsqrt(mean + EPS), (32, 128))
        for j in range(D // 128):
            v = rows_v[at, j * 128 : (j + 1) * 128].astype(F32)
            nrm[at, j * 128 : (j + 1) * 128] = (v * inv * gain_v[:, j * 128 : (j + 1) * 128]).astype(BF16)
        return carry

    lax.fori_loop(0, 5, norm, 0)

    pl.semaphore_wait(barrier, 64)

    def send_page(q, t):
        push(sx.at[q, lax.div(t, 2)], kv.at[c, 16 * r + chip], zs_s.at[0], zs_r.at[r], (q, 2 * t + c))

    pltpu.make_async_copy(sx.at[r, k], kv.at[c, 16 * r + chip], zs_r.at[r]).start()

    ld_wk.wait()
    part[0:ROWS, :] = jnp.zeros((ROWS, HD), F32)

    for i in range(8):
        cols = slice(1024 * i, 1024 * (i + 1))
        others(send_page, 8 * i, 8 * i + 8)
        part[0:ROWS, :] += nt_dot(nrm[:, cols], wk_v[:, cols])
    kvp[...] = part[0:ROWS, :].astype(BF16)
    ld_wo = load(wo_hbm, wo_v, 12)
    head_to = lax.div(lax.rem(m, 16), 2)
    fr_slot = 2 * c + lax.div(m, 16)
    for i in range(2):
        t = 2 * head_to + i

        @pl.when(t == chip)
        def _():
            pltpu.make_async_copy(kvp, fr.at[fr_slot], fr_r.at[0]).start()

        @pl.when(t != chip)
        def _():
            push(kvp, fr.at[fr_slot], fr_s.at[0], fr_r.at[0], (r, 2 * t + c))

    acc[...] = jnp.zeros((ROWS, 2 * HD), F32)
    for i in range(4):
        ld_wq[i].wait()

        def q_step(j, carry):
            at = pl.multiple_of(2048 * i + 1024 * j, 1024)
            acc[...] += nn_dot(nrm[:, pl.ds(at, 1024)], wq_v[pl.ds(at, 1024), :])
            return carry

        lax.fori_loop(0, 2, q_step, 0)
    q2[0:ROWS, :] = acc[:, 0:HD].astype(BF16)
    q2[ROWS : 2 * ROWS, :] = acc[:, HD : 2 * HD].astype(BF16)

    own_picked = picked[r].astype(F32)
    cols = [to_column(own_picked[s : s + 1, :]) + 512.0 * s for s in range(SPANS)]
    question = lax.broadcasted_iota(jnp.int32, (64, 1), 0).astype(F32)
    own_len = qlen[r].astype(F32)
    row_pos = jnp.concatenate(cols + [question + float(KEYS)], axis=0)
    key_col = jnp.concatenate(cols + [jnp.where(question < own_len, question + float(KEYS), FAR)], axis=0)
    eye = lax.broadcasted_iota(jnp.int32, (ROWS, 256), 0) == lax.broadcasted_iota(jnp.int32, (ROWS, 256), 1)
    fresh_pos = jnp.sum(jnp.where(eye, jnp.broadcast_to(key_col, (ROWS, 256)), 0.0), axis=0, keepdims=True)
    fresh_pos = jnp.where(lax.broadcasted_iota(jnp.int32, (1, 256), 1) < ROWS, fresh_pos, FAR)
    row_pos_b = jnp.broadcast_to(row_pos, (ROWS, 256))
    picked_b = row_pos_b[0 : SPANS * RCH]

    own_half = fr.at[pl.ds(2 * c, 2)]
    wait_all(own_half, fr_r.at[0])
    push(own_half, own_half, fr_s.at[1], fr_r.at[1], sib)
    wait_all(fr.at[pl.ds(2 - 2 * c, 2)], fr_r.at[1])
    row = lax.broadcasted_iota(jnp.int32, (SPANS * RCH, 256), 0)
    wanted = by_index(lax.div(row, RCH), span_of) * RCH + lax.rem(row, RCH)
    pick_rows = jnp.where(lax.broadcasted_iota(jnp.int32, (SPANS * RCH, 256), 1) == wanted, 1.0, 0.0).astype(BF16)
    by_holder = []
    for s in range(2):
        fk[s, 0:ROWS, :] = (fr[s].astype(F32) + fr[2 + s].astype(F32)).astype(BF16)
        fk[s, ROWS:256, :] = jnp.zeros((256 - ROWS, HD), BF16)
        by_holder.append(nn_dot(pick_rows, fk[s]))
    for x in range(4):
        sj[x] = jnp.concatenate([b[x * RCH : (x + 1) * RCH] for b in by_holder], axis=0).astype(BF16)
    rj_half = lax.div(r, 2)
    rj_slot = lax.rem(r, 2)

    @pl.when(rj_half == c)
    def _():
        for d in (2, 1, 3):
            x = lax.rem(r + d, 4)
            push(sj.at[x], rj1.at[rj_slot], js_s.at[0], js_r.at[rj_slot], (x, m))
        rj1[rj_slot] = sj[r]

    def score(at, keys, key_pos):
        s = nt_dot(q2[...], keys) * SCALE
        seen = row_pos_b >= jnp.broadcast_to(key_pos, (ROWS, 256))
        for half in range(2):
            rows = slice(half * ROWS, (half + 1) * ROWS)
            masked = jnp.where(seen, s[rows], NEG)
            scores[at, rows, :] = masked
            peak[rows, :] = jnp.maximum(peak[rows, :], jnp.maximum(masked[:, :128], masked[:, 128:]))

    peak[...] = jnp.full((2 * ROWS, 128), NEG, F32)
    score(8, fk[0], fresh_pos)

    lane = lax.broadcasted_iota(jnp.int32, (1, 256), 1)
    lane_pos = (lane >> 4) * 32 + (lane & 15)

    def page_keys(cc, x):
        span = jnp.where(x == 0, span_of[0], jnp.where(x == 1, span_of[1], jnp.where(x == 2, span_of[2], span_of[3])))
        pos = (lane_pos + (span * 512 + cc * 16)).astype(F32)
        same = picked_b == jnp.broadcast_to(pos, (SPANS * RCH, 256))
        gone = jnp.max(jnp.where(same, 1.0, 0.0), axis=0, keepdims=True)
        return jnp.where(gone > 0.5, FAR, pos)

    def group(cc, x):
        return kv.at[cc, pl.ds(16 * x, 16)]

    for d in (2, 1, 3, 0):
        x = lax.rem(r + d, 4)
        wait_all(group(c, x), zs_r.at[x])
        push(group(c, x), group(c, x), cs_s.at[0], cs_r.at[x], sib)

    def page_part(cc, x, s):
        return kv[cc, pl.ds(16 * x, 16), s].reshape(256, HD)

    def own_scores(x, carry):
        score(x, page_part(c, x, 0), page_keys(c, x))
        return carry

    lax.fori_loop(0, 4, own_scores, 0)

    def sib_scores(x, carry):
        wait_all(group(1 - c, x), cs_r.at[x])
        score(4 + x, page_part(1 - c, x, 0), page_keys(1 - c, x))
        return carry

    lax.fori_loop(0, 4, sib_scores, 0)

    for q in range(2):

        @pl.when(r != 2 * c + q)
        def _():
            wait_all(rj1.at[q], js_r.at[q])

    rj[c, k] = rj1[...]

    def spread_fresh(d, carry):
        t = lax.rem(k + d, 8)
        push(rj1, rj.at[c, k], jz_s.at[0], jz_r.at[0], (r, (2 * t + lax.rem(y, 2)) * 2 + c))
        return carry

    lax.fori_loop(1, 8, spread_fresh, 0)

    peak[...] = jnp.broadcast_to(jnp.max(peak[...], axis=1, keepdims=True), (2 * ROWS, 128))
    total[...] = jnp.zeros((2 * ROWS, 128), F32)
    part[...] = jnp.zeros((2 * ROWS, HD), F32)

    def weigh(at, vals):
        top = peak[...]
        w0 = jnp.exp(scores[at, :, 0:128] - top)
        w1 = jnp.exp(scores[at, :, 128:256] - top)
        total[...] += w0 + w1
        part[...] += nn_dot(jnp.concatenate([w0, w1], axis=1).astype(BF16), vals)

    def page_values(i, carry):
        far = lax.div(i, 4)
        weigh(i, page_part(c + far * (1 - 2 * c), lax.rem(i, 4), 1))
        return carry

    lax.fori_loop(0, 8, page_values, 0)
    weigh(8, fk[1])
    att = part[...] / jnp.sum(total[...], axis=1, keepdims=True)
    gath[c, chip, :, 0:HD] = att[0:ROWS].astype(BF16)
    gath[c, chip, :, HD : 2 * HD] = att[ROWS : 2 * ROWS].astype(BF16)

    def chip_at(cc, df, ds):
        f = lax.rem(y * (1 - cc) + z * cc + df, 4)
        s = lax.rem(z * (1 - cc) + y * cc + ds, 4)
        return (4 * s + f) * (1 - cc) + (4 * f + s) * cc

    def forward(block, df, ds):
        ref = gath.at[c, block]
        push(ref, ref, g_s.at[0], g_r.at[block], (r, 2 * chip_at(c, df, ds) + c))

    def across(block):
        ref = gath.at[c, block]
        push(ref, ref, gc_s.at[0], gc_r.at[block], sib)

    def arrived(block):
        wait_all(gath.at[c, block], g_r.at[block])

    def project(cc, ds):
        more = jnp.zeros((ROWS, 2 * HD), F32)
        for df in LINE:
            block = chip_at(cc, df, ds)
            at = pl.multiple_of((2 * block + cc) * 256, 256)
            more = more + nn_dot(gath[cc, block], wo_v[pl.ds(at, 256), :])
        acc[...] += more

    def crossed(ds):
        for df in LINE:
            block = chip_at(1 - c, df, ds)
            wait_all(gath.at[1 - c, block], gc_r.at[block])

    for df in (2, 1, 3):
        forward(chip, df, 0)
    for ds in (2, 1, 3):
        forward(chip, 0, ds)
    across(chip)
    acc[...] = jnp.zeros((ROWS, 2 * HD), F32)

    for df in (1, 3, 2):
        block = chip_at(c, df, 0)
        arrived(block)
        for ds in (2, 1, 3) if df == 2 else (1, 3):
            forward(block, 0, ds)
        across(block)
    ld_wo.wait()
    project(c, 0)
    wait_all(rj.at[c, pl.ds(0, 7)], jz_r.at[0])
    push(rj.at[c], rj.at[c], jz_s.at[1], jz_r.at[1], sib)
    for df, ds in ((0, 1), (0, 3), (1, 3), (3, 1), (1, 1), (3, 3), (2, 1), (2, 3), (0, 2)):
        block = chip_at(c, df, ds)
        arrived(block)
        if (df, ds) in ((1, 3), (3, 1)):
            forward(block, 0, 4 - ds)
        across(block)
    crossed(0)
    project(1 - c, 0)
    project(c, 1)
    project(c, 3)

    wait_all(rj.at[1 - c], jz_r.at[1])
    col = lax.broadcasted_iota(jnp.int32, (RCH, 192), 1)
    col_req = lax.div(col, 48)
    col_in = lax.rem(col, 48)
    row_in = lax.broadcasted_iota(jnp.int32, (RCH, 192), 0)
    target = jnp.zeros((1, 192), F32)
    low = (m * 16).astype(F32)
    for q in range(4):
        pq = picked[q].astype(F32)
        mine = jnp.zeros((1, RCH), F32)
        for s in range(SPANS):
            mine = mine + jnp.where(send_span[q] == s, pq[s : s + 1, :], 0.0)
        mine = mine - low
        mine = jnp.where((mine >= 0.0) & (mine < 16.0), mine + (send_slot[q] * 16).astype(F32), -1.0)
        fits = (col_req == q) & ((col_in == row_in) | (col_in == row_in + RCH))
        target = target + jnp.sum(
            jnp.where(fits, jnp.broadcast_to(to_column(mine), (RCH, 192)), 0.0), axis=0, keepdims=True
        )
    line = lax.broadcasted_iota(jnp.int32, (128, 192), 0).astype(F32)
    is_key = lax.rem(lax.broadcasted_iota(jnp.int32, (128, 192), 1), 48) < RCH
    match = line == jnp.broadcast_to(target, (128, 192))
    pick_key = jnp.where(match & is_key, 1.0, 0.0)
    pick_val = jnp.where(match & jnp.logical_not(is_key), 1.0, 0.0)
    hit = jnp.broadcast_to(jnp.max(pick_key, axis=1, keepdims=True), (128, HD)) > 0.5
    pick = jnp.concatenate([pick_key, pick_val], axis=0).astype(BF16)
    for h in range(KVH):
        new = nn_dot(pick[:, 0:96], rj[0, h].reshape(96, HD)) + nn_dot(pick[:, 96:192], rj[1, h].reshape(96, HD))
        for s in range(2):
            at = slice(1024 * s + h * HD, 1024 * s + (h + 1) * HD)
            old = pool_v[:, :, at].astype(F32).reshape(128, HD)
            joined_v[:, :, at] = (
                jnp.where(hit, new[128 * s : 128 * (s + 1)], old).astype(BF16).reshape(8, 16, HD)
            )

    crossed(1)
    project(1 - c, 1)
    crossed(3)
    project(1 - c, 3)
    for df in (2, 1, 3):
        block = chip_at(c, df, 2)
        arrived(block)
        across(block)
    project(c, 2)
    crossed(2)
    project(1 - c, 2)
    live = lax.broadcasted_iota(jnp.int32, (ROWS, 2 * HD), 0) < SPANS * RCH + qlen[r]
    out_ref[0] = jnp.where(live, acc[...], 0.0).astype(BF16)

    wait_all(kv.at[0, pl.ds(0, 63)], zs_s.at[0])
    wait_all(kv.at[0], cs_s.at[0])

    wait_all(own_half, fr_s.at[1])

    @pl.when(head_to == k)
    def _():
        wait_all(fr.at[pl.ds(0, 1)], fr_s.at[0])

    @pl.when(head_to != k)
    def _():
        wait_all(fr.at[pl.ds(0, 2)], fr_s.at[0])


    @pl.when(rj_half == c)
    def _():
        wait_all(sj.at[pl.ds(0, 3)], js_s.at[0])

    wait_all(rj.at[0, pl.ds(0, 7)], jz_s.at[0])
    wait_all(rj.at[0], jz_s.at[1])
    wait_all(gath.at[0, pl.ds(0, 15)], g_s.at[0])
    wait_all(gath.at[0], gc_s.at[0])


def finish(attn, joined, attn_out, joined_out, sems):
    copies = [
        pltpu.make_async_copy(joined, joined_out, sems.at[0]),
        pltpu.make_async_copy(attn, attn_out, sems.at[1]),
    ]
    for cp in copies:
        cp.start()
    for cp in copies:
        cp.wait()


def local(
    rows_in, norm_gain, w_query, w_keyval, w_out, page_pool, stretch_ids, page_slot, picked, question_len
):
    any_spec = pl.BlockSpec(memory_space=pl.ANY)
    smem = pl.BlockSpec(memory_space=pltpu.SMEM)
    vmem = pl.BlockSpec(memory_space=pltpu.VMEM)
    sem = pltpu.SemaphoreType.DMA
    attn, joined = pl.pallas_call(
        kernel,
        out_shape=(pltpu.VMEM((1, ROWS, 2 * HD), BF16), pltpu.VMEM(page_pool.shape, BF16)),
        in_specs=[any_spec] * 6 + [smem, smem, vmem, smem],
        out_specs=(vmem, vmem),
        scratch_shapes=[
            pltpu.VMEM((ROWS, D), BF16),
            pltpu.VMEM((1, D), F32),
            pltpu.VMEM((ROWS, D), BF16),
            pltpu.VMEM((D, 2 * HD), BF16),
            pltpu.VMEM((HD, D), BF16),
            pltpu.VMEM((D, 2 * HD), BF16),
            pltpu.VMEM((8, 16, 2048), BF16),
            pltpu.VMEM((4, KVH, 2, 16, HD), BF16),
            pltpu.VMEM((2, 64, 2, 16, HD), BF16),
            pltpu.VMEM((ROWS, HD), BF16),
            pltpu.VMEM((4, ROWS, HD), BF16),
            pltpu.VMEM((2, 256, HD), BF16),
            pltpu.VMEM((2 * ROWS, HD), BF16),
            pltpu.VMEM((9, 2 * ROWS, 256), F32),
            pltpu.VMEM((2 * ROWS, 128), F32),
            pltpu.VMEM((2 * ROWS, 128), F32),
            pltpu.VMEM((2 * ROWS, HD), F32),
            pltpu.VMEM((2, 16, ROWS, 2 * HD), BF16),
            pltpu.VMEM((ROWS, 2 * HD), F32),
            pltpu.VMEM((4, 2 * RCH, HD), BF16),
            pltpu.VMEM((2, 2 * RCH, HD), BF16),
            pltpu.VMEM((2, KVH, 2, 2 * RCH, HD), BF16),
            sem((13,)),
            sem((1,)),
            sem((4,)),
            sem((1,)),
            sem((4,)),
            sem((2,)),
            sem((2,)),
            sem((1,)),
            sem((2,)),
            sem((2,)),
            sem((2,)),
            sem((1,)),
            sem((16,)),
            sem((1,)),
            sem((16,)),
        ],
        compiler_params=pltpu.CompilerParams(
            collective_id=0, has_side_effects=True, vmem_limit_bytes=56 * 1024 * 1024
        ),
        name="joined_attention",
    )(
        rows_in,
        norm_gain.reshape(1, D),
        w_query,
        w_keyval.T,
        w_out,
        page_pool,
        stretch_ids,
        page_slot,
        picked,
        question_len,
    )
    return pl.pallas_call(
        finish,
        out_shape=(
            jax.ShapeDtypeStruct(attn.shape, BF16),
            jax.ShapeDtypeStruct(joined.shape, BF16),
        ),
        in_specs=[vmem, vmem],
        out_specs=(any_spec, any_spec),
        scratch_shapes=[sem((2,))],
        name="write_out",
    )(pltpu.with_memory_space_constraint(attn, pltpu.VMEM), pltpu.with_memory_space_constraint(joined, pltpu.VMEM))


def solution(mesh):
    in_specs = (
        P("req", None, None),
        P(),
        P(None, "grp"),
        P(None, "grp"),
        P(None, "grp"),
        P("req", "grp", None),
        P(),
        P(),
        P(),
        P(),
    )
    out_specs = (P("req", None, "grp"), P("req", "grp", None))
    return jax.shard_map(local, mesh=mesh, in_specs=in_specs, out_specs=out_specs, check_vma=False)
```

```python
import functools
import math

import jax
import jax.numpy as jnp
from jax import lax
from jax.experimental import pallas as pl
from jax.experimental.pallas import tpu as pltpu
from jax.sharding import PartitionSpec as P

MESH = pl.DeviceIdType.MESH
F32 = jnp.float32
BF16 = jnp.bfloat16
HD = 128
KVH = 8
ROWS = 160
RCH = 24
SPANS = 4
D = 8192
KEYS = 2048
EPS = 1e-05
EXP2_SCALE = math.log2(math.e) / math.sqrt(HD)
NEG = -1e30
FAR = 1e9
LINE = (0, 1, 3, 2)
HOPS = (0, 1, 2, 1)
FARTHEST_FIRST = sorted(
    [(n // 16, n // 4 % 4, n % 4) for n in range(1, 64)], key=lambda steps: -sum(HOPS[d] for d in steps)
)


def nt_dot(a, b):
    return lax.dot_general(a, b, (((1,), (1,)), ((), ())), preferred_element_type=F32)


def nn_dot(a, b):
    return jnp.dot(a, b, preferred_element_type=F32)


def by_index(index, values):
    low = jnp.where(index == 0, values[0], values[1])
    return jnp.where(index < 2, low, jnp.where(index == 2, values[2], values[3]))


def to_column(row):
    n = row.shape[1]
    eye = lax.broadcasted_iota(jnp.int32, (n, n), 0) == lax.broadcasted_iota(jnp.int32, (n, n), 1)
    return jnp.sum(jnp.where(eye, jnp.broadcast_to(row, (n, n)), 0.0), axis=1, keepdims=True)


def kernel(
    rows_hbm,
    gain_hbm,
    wq_hbm,
    wk_hbm,
    wo_hbm,
    pool_hbm,
    ids,
    slots,
    picked,
    qlen,
    out_ref,
    joined_v,
    rows_v,
    gain_v,
    nrm,
    wq_v,
    wk_v,
    wo_v,
    pool_v,
    sx,
    kv,
    kvp,
    fr,
    fk,
    q2,
    scores,
    peak,
    gath,
    acc,
    sj,
    rj1,
    rj,
    ld,
    zs_s,
    zs_r,
    cs_s,
    cs_r,
    fr_s,
    fr_r,
    js_s,
    js_r,
    jz_s,
    jz_r,
    g_s,
    g_r,
    gc_s,
    gc_r,
):
    r = lax.axis_index("req")
    m = lax.axis_index("grp")
    z = lax.div(m, 8)
    y = lax.rem(lax.div(m, 2), 4)
    c = lax.rem(m, 2)
    chip = lax.div(m, 2)
    k = lax.div(m, 4)
    sib = (r, m + 1 - 2 * c)

    def load(src, dst, i):
        cp = pltpu.make_async_copy(src, dst, ld.at[i])
        cp.start()
        return cp

    def push(src, dst, send, recv, dev):
        pltpu.make_async_remote_copy(
            src_ref=src, dst_ref=dst, send_sem=send, recv_sem=recv, device_id=dev, device_id_type=MESH
        ).start()

    def wait_all(ref, sem):
        pltpu.make_async_copy(ref, ref, sem).wait()

    barrier = pltpu.get_barrier_semaphore()

    def others(act, first=0, last=63):
        for dx, dy, dz in FARTHEST_FIRST[first:last]:
            act(lax.rem(r + dx, 4), 4 * lax.rem(z + dz, 4) + lax.rem(y + dy, 4))

    def greet(q, t):
        pl.semaphore_signal(barrier, inc=1, device_id=(q, 2 * t + c), device_id_type=MESH)

    others(greet)
    pl.semaphore_signal(barrier, inc=1, device_id=sib, device_id_type=MESH)

    for i in range(5):
        load(rows_hbm.at[0, pl.ds(32 * i, 32)], rows_v.at[pl.ds(32 * i, 32)], 1 + i)
    ld_gain = load(gain_hbm, gain_v, 6)
    ld_pool = load(pool_hbm, pool_v, 0)
    ld_wk = load(wk_hbm, wk_v.at[pl.ds(pl.multiple_of(64 * c, 64), 64)], 7)

    wk_v[pl.ds(pl.multiple_of(64 - 64 * c, 64), 64), :] = jnp.zeros((64, D), BF16)

    place = [[slots[ids[q, s]] for s in range(SPANS)] for q in range(4)]
    send_slot, send_span = [], []
    for q in range(4):
        slot_q, span_q = 0, 0
        for s in range(SPANS):
            here = (place[q][s] >> 3) == r
            slot_q = slot_q + jnp.where(here, place[q][s] & 7, 0)
            span_q = span_q + jnp.where(here, s, 0)
        send_slot.append(slot_q)
        send_span.append(span_q)
    own_place = [slots[ids[r, s]] for s in range(SPANS)]
    span_of = []
    for x in range(4):
        span_x = 0
        for s in range(SPANS):
            span_x = span_x + jnp.where((own_place[s] >> 3) == x, s, 0)
        span_of.append(span_x)

    ld_pool.wait()
    row = lax.broadcasted_iota(jnp.int32, (64, 128), 0)
    wanted = by_index(row >> 4, send_slot) * 16 + (row & 15)
    pick_page = jnp.where(lax.broadcasted_iota(jnp.int32, (64, 128), 1) == wanted, 1.0, 0.0).astype(BF16)
    for h in range(2 * KVH):
        piece = nn_dot(pick_page, pool_v[:, :, h * HD : (h + 1) * HD].reshape(128, HD)).astype(BF16)
        for q in range(4):
            sx[q, h % KVH, h // KVH] = piece[16 * q : 16 * (q + 1)]
    ld_gain.wait()

    def norm(i, carry):
        at = pl.ds(pl.multiple_of(32 * i, 32), 32)
        wait_all(rows_v.at[at], ld.at[1 + i])
        squares = jnp.zeros((32, 128), F32)
        for j in range(D // 128):
            v = rows_v[at, j * 128 : (j + 1) * 128].astype(F32)
            squares = squares + v * v
        mean = jnp.sum(squares, axis=1, keepdims=True) * (1.0 / D)
        inv = jnp.broadcast_to(lax.rsqrt(mean + EPS), (32, 128))
        for j in range(D // 128):
            v = rows_v[at, j * 128 : (j + 1) * 128].astype(F32)
            nrm[at, j * 128 : (j + 1) * 128] = (v * inv * gain_v[:, j * 128 : (j + 1) * 128]).astype(BF16)
        return carry

    lax.fori_loop(0, 5, norm, 0)

    ld_wq = [
        load(wq_hbm.at[pl.ds(1024 * i, 1024)], wq_v.at[pl.ds(1024 * i, 1024)], 8 + i) for i in range(8)
    ]

    ld_wk.wait()
    new_kv = jnp.zeros((ROWS, HD), F32)
    for i in range(8):
        cols = slice(1024 * i, 1024 * (i + 1))
        new_kv = new_kv + nt_dot(nrm[:, cols], wk_v[:, cols])
    kvp[...] = new_kv.astype(BF16)
    pl.semaphore_wait(barrier, 64)
    head_to = lax.div(lax.rem(m, 16), 2)
    fr_slot = 2 * c + lax.div(m, 16)
    for i in range(2):
        t = 2 * head_to + i

        @pl.when(t == chip)
        def _():
            pltpu.make_async_copy(kvp, fr.at[fr_slot], fr_r.at[0]).start()

        @pl.when(t != chip)
        def _():
            push(kvp, fr.at[fr_slot], fr_s.at[0], fr_r.at[0], (r, 2 * t + c))

    def send_page(q, t):
        push(sx.at[q, lax.div(t, 2)], kv.at[c, 16 * r + chip], zs_s.at[0], zs_r.at[r], (q, 2 * t + c))

    pltpu.make_async_copy(sx.at[r, k], kv.at[c, 16 * r + chip], zs_r.at[r]).start()

    pl.when(m >= 0)(functools.partial(others, send_page))
    query = jnp.zeros((ROWS, 2 * HD), F32)
    for i in range(8):
        ld_wq[i].wait()
        at = slice(1024 * i, 1024 * (i + 1))
        query = query + nn_dot(nrm[:, at], wq_v[at, :])
    q2[0:ROWS, :] = query[:, 0:HD].astype(BF16)
    q2[ROWS : 2 * ROWS, :] = query[:, HD : 2 * HD].astype(BF16)

    own_half = fr.at[pl.ds(2 * c, 2)]
    wait_all(own_half, fr_r.at[0])
    push(own_half, own_half, fr_s.at[1], fr_r.at[1], sib)
    ld_wo = load(wo_hbm, wo_v, 16)

    own_picked = picked[r].astype(F32)
    cols = [to_column(own_picked[s : s + 1, :]) + 512.0 * s for s in range(SPANS)]
    question = lax.broadcasted_iota(jnp.int32, (64, 1), 0).astype(F32)
    own_len = qlen[r].astype(F32)
    row_pos = jnp.concatenate(cols + [question + float(KEYS)], axis=0)
    key_col = jnp.concatenate(cols + [jnp.where(question < own_len, question + float(KEYS), FAR)], axis=0)
    eye = lax.broadcasted_iota(jnp.int32, (ROWS, 256), 0) == lax.broadcasted_iota(jnp.int32, (ROWS, 256), 1)
    fresh_pos = jnp.sum(jnp.where(eye, jnp.broadcast_to(key_col, (ROWS, 256)), 0.0), axis=0, keepdims=True)
    fresh_pos = jnp.where(lax.broadcasted_iota(jnp.int32, (1, 256), 1) < ROWS, fresh_pos, FAR)
    row_pos_b = jnp.broadcast_to(row_pos, (ROWS, 256))
    picked_b = row_pos_b[0 : SPANS * RCH]

    wait_all(fr.at[pl.ds(2 - 2 * c, 2)], fr_r.at[1])
    row = lax.broadcasted_iota(jnp.int32, (SPANS * RCH, 256), 0)
    wanted = by_index(lax.div(row, RCH), span_of) * RCH + lax.rem(row, RCH)
    pick_rows = jnp.where(lax.broadcasted_iota(jnp.int32, (SPANS * RCH, 256), 1) == wanted, 1.0, 0.0).astype(BF16)
    by_holder = []
    for s in range(2):
        fk[s, 0:ROWS, :] = (fr[s].astype(F32) + fr[2 + s].astype(F32)).astype(BF16)
        fk[s, ROWS:256, :] = jnp.zeros((256 - ROWS, HD), BF16)
        by_holder.append(nn_dot(pick_rows, fk[s]))
    for x in range(4):
        sj[x] = jnp.concatenate([b[x * RCH : (x + 1) * RCH] for b in by_holder], axis=0).astype(BF16)
    rj_half = lax.div(r, 2)
    rj_slot = lax.rem(r, 2)

    @pl.when(rj_half == c)
    def _():
        for d in (2, 1, 3):
            x = lax.rem(r + d, 4)
            push(sj.at[x], rj1.at[rj_slot], js_s.at[0], js_r.at[rj_slot], (x, m))
        rj1[rj_slot] = sj[r]

    def score(at, keys, key_pos):
        s = nt_dot(q2[...], keys)
        seen = row_pos_b >= jnp.broadcast_to(key_pos, (ROWS, 256))
        for half in range(2):
            rows = slice(half * ROWS, (half + 1) * ROWS)
            masked = jnp.where(seen, s[rows], NEG)
            scores[at, rows, :] = masked
            peak[rows, :] = jnp.maximum(peak[rows, :], jnp.maximum(masked[:, :128], masked[:, 128:]))

    peak[...] = jnp.full((2 * ROWS, 128), NEG, F32)
    score(8, fk[0], fresh_pos)

    def group(cc, x):
        return kv.at[cc, pl.ds(16 * x, 16)]

    for d in (2, 1, 3, 0):
        x = lax.rem(r + d, 4)
        wait_all(group(c, x), zs_r.at[x])
        push(group(c, x), group(c, x), cs_s.at[0], cs_r.at[x], sib)

    for q in range(2):

        @pl.when(r != 2 * c + q)
        def _():
            wait_all(rj1.at[q], js_r.at[q])

    rj[c, k] = rj1[...]

    def spread_fresh(d, carry):
        t = lax.rem(k + d, 8)
        push(rj1, rj.at[c, k], jz_s.at[0], jz_r.at[0], (r, (2 * t + lax.rem(y, 2)) * 2 + c))
        return carry

    lax.fori_loop(1, 8, spread_fresh, 0)

    lane = lax.broadcasted_iota(jnp.int32, (1, 256), 1)
    lane_pos = (lane >> 4) * 32 + (lane & 15)

    def page_keys(cc, x):
        span = jnp.where(x == 0, span_of[0], jnp.where(x == 1, span_of[1], jnp.where(x == 2, span_of[2], span_of[3])))
        pos = (lane_pos + (span * 512 + cc * 16)).astype(F32)
        same = picked_b == jnp.broadcast_to(pos, (SPANS * RCH, 256))
        gone = jnp.max(jnp.where(same, 1.0, 0.0), axis=0, keepdims=True)
        return jnp.where(gone > 0.5, FAR, pos)

    def page_part(cc, x, s):
        return kv[cc, pl.ds(16 * x, 16), s].reshape(256, HD)

    for x in range(4):
        score(4 * c + x, page_part(c, x, 0), page_keys(c, x))

    for x in range(4):
        wait_all(group(1 - c, x), cs_r.at[x])
        score(4 * (1 - c) + x, page_part(1 - c, x, 0), page_keys(1 - c, x))

    for h in range(2):
        rows = slice(h * ROWS, (h + 1) * ROWS)
        top = jnp.broadcast_to(jnp.max(peak[rows, :], axis=1, keepdims=True), (ROWS, 128))
        total = jnp.zeros((ROWS, 128), F32)
        mixed = jnp.zeros((ROWS, HD), F32)
        for i in range(9):
            w0 = jnp.exp2((scores[i, rows, 0:128] - top) * EXP2_SCALE)
            w1 = jnp.exp2((scores[i, rows, 128:256] - top) * EXP2_SCALE)
            total = total + (w0 + w1)
            vals = fk[1] if i == 8 else page_part(i // 4, i % 4, 1)
            mixed = mixed + nn_dot(jnp.concatenate([w0, w1], axis=1).astype(BF16), vals)
        att = mixed / jnp.sum(total, axis=1, keepdims=True)
        gath[c, chip, :, h * HD : (h + 1) * HD] = att.astype(BF16)

    def chip_at(cc, df, ds):
        f = lax.rem(y * (1 - cc) + z * cc + df, 4)
        s = lax.rem(z * (1 - cc) + y * cc + ds, 4)
        return (4 * s + f) * (1 - cc) + (4 * f + s) * cc

    def forward(block, df, ds):
        ref = gath.at[c, block]
        push(ref, ref, g_s.at[0], g_r.at[block], (r, 2 * chip_at(c, df, ds) + c))

    def across(block):
        ref = gath.at[c, block]
        push(ref, ref, gc_s.at[0], gc_r.at[block], sib)

    def arrived(block):
        wait_all(gath.at[c, block], g_r.at[block])

    def project(cc, ds):
        more = jnp.zeros((ROWS, 2 * HD), F32)
        for df in LINE:
            block = chip_at(cc, df, ds)
            at = pl.multiple_of((2 * block + cc) * 256, 256)
            more = more + nn_dot(gath[cc, block], wo_v[pl.ds(at, 256), :])
        acc[...] += more

    def crossed(ds):
        for df in LINE:
            block = chip_at(1 - c, df, ds)
            wait_all(gath.at[1 - c, block], gc_r.at[block])

    for df in (1, 3, 2):
        forward(chip, df, 0)
    across(chip)
    for ds in (1, 3):
        forward(chip, 0, ds)
    acc[...] = jnp.zeros((ROWS, 2 * HD), F32)
    for df in (1, 3, 2):
        block = chip_at(c, df, 0)
        arrived(block)
        for ds in (2, 1, 3) if df == 2 else (1, 3):
            forward(block, 0, ds)
        across(block)
        if df == 3:
            forward(chip, 0, 2)
    ld_wo.wait()
    project(c, 0)
    for df, ds in ((0, 1), (0, 3), (1, 3), (3, 1), (1, 1), (3, 3), (2, 1), (2, 3), (0, 2)):
        block = chip_at(c, df, ds)
        arrived(block)
        if (df, ds) in ((1, 3), (3, 1)):
            forward(block, 0, 4 - ds)
        across(block)
    crossed(0)
    wait_all(rj.at[c, pl.ds(0, 7)], jz_r.at[0])
    push(rj.at[c], rj.at[c], jz_s.at[1], jz_r.at[1], sib)
    project(1 - c, 0)
    project(c, 1)
    project(c, 3)

    crossed(1)
    project(1 - c, 1)
    crossed(3)
    project(1 - c, 3)
    for df in (2, 1, 3):
        block = chip_at(c, df, 2)
        arrived(block)
        across(block)
    project(c, 2)
    wait_all(rj.at[1 - c], jz_r.at[1])
    col = lax.broadcasted_iota(jnp.int32, (RCH, 192), 1)
    col_req = lax.div(col, 48)
    col_in = lax.rem(col, 48)
    row_in = lax.broadcasted_iota(jnp.int32, (RCH, 192), 0)
    target = jnp.zeros((1, 192), F32)
    low = (m * 16).astype(F32)
    for q in range(4):
        pq = picked[q].astype(F32)
        mine = jnp.zeros((1, RCH), F32)
        for s in range(SPANS):
            mine = mine + jnp.where(send_span[q] == s, pq[s : s + 1, :], 0.0)
        mine = mine - low
        mine = jnp.where((mine >= 0.0) & (mine < 16.0), mine + (send_slot[q] * 16).astype(F32), -1.0)
        fits = (col_req == q) & ((col_in == row_in) | (col_in == row_in + RCH))
        target = target + jnp.sum(
            jnp.where(fits, jnp.broadcast_to(to_column(mine), (RCH, 192)), 0.0), axis=0, keepdims=True
        )
    line = lax.broadcasted_iota(jnp.int32, (128, 192), 0).astype(F32)
    is_key = lax.rem(lax.broadcasted_iota(jnp.int32, (128, 192), 1), 48) < RCH
    match = line == jnp.broadcast_to(target, (128, 192))
    pick_key = jnp.where(match & is_key, 1.0, 0.0)
    pick_val = jnp.where(match & jnp.logical_not(is_key), 1.0, 0.0)
    hit = jnp.broadcast_to(jnp.max(pick_key, axis=1, keepdims=True), (128, HD)) > 0.5
    pick = jnp.concatenate([pick_key, pick_val], axis=0).astype(BF16)
    for h in range(KVH):
        new = nn_dot(pick[:, 0:96], rj[0, h].reshape(96, HD)) + nn_dot(pick[:, 96:192], rj[1, h].reshape(96, HD))
        for s in range(2):
            at = slice(1024 * s + h * HD, 1024 * s + (h + 1) * HD)
            old = pool_v[:, :, at].astype(F32).reshape(128, HD)
            joined_v[:, :, at] = (
                jnp.where(hit, new[128 * s : 128 * (s + 1)], old).astype(BF16).reshape(8, 16, HD)
            )

    crossed(2)
    project(1 - c, 2)
    live = lax.broadcasted_iota(jnp.int32, (ROWS, 2 * HD), 0) < SPANS * RCH + qlen[r]
    out_ref[0] = jnp.where(live, acc[...], 0.0).astype(BF16)

    wait_all(kv.at[0, pl.ds(0, 63)], zs_s.at[0])
    wait_all(kv.at[0], cs_s.at[0])

    wait_all(own_half, fr_s.at[1])

    @pl.when(head_to == k)
    def _():
        wait_all(fr.at[pl.ds(0, 1)], fr_s.at[0])

    @pl.when(head_to != k)
    def _():
        wait_all(fr.at[pl.ds(0, 2)], fr_s.at[0])


    @pl.when(rj_half == c)
    def _():
        wait_all(sj.at[pl.ds(0, 3)], js_s.at[0])

    wait_all(rj.at[0, pl.ds(0, 7)], jz_s.at[0])
    wait_all(rj.at[0], jz_s.at[1])
    wait_all(gath.at[0, pl.ds(0, 15)], g_s.at[0])
    wait_all(gath.at[0], gc_s.at[0])


def finish(attn, joined, attn_out, joined_out, sems):
    copies = [
        pltpu.make_async_copy(joined, joined_out, sems.at[0]),
        pltpu.make_async_copy(attn, attn_out, sems.at[1]),
    ]
    for cp in copies:
        cp.start()
    for cp in copies:
        cp.wait()


def local(
    rows_in, norm_gain, w_query, w_keyval, w_out, page_pool, stretch_ids, page_slot, picked, question_len
):
    any_spec = pl.BlockSpec(memory_space=pl.ANY)
    smem = pl.BlockSpec(memory_space=pltpu.SMEM)
    vmem = pl.BlockSpec(memory_space=pltpu.VMEM)
    sem = pltpu.SemaphoreType.DMA
    attn, joined = pl.pallas_call(
        kernel,
        out_shape=(pltpu.VMEM((1, ROWS, 2 * HD), BF16), pltpu.VMEM(page_pool.shape, BF16)),
        in_specs=[any_spec] * 6 + [smem, smem, vmem, smem],
        out_specs=(vmem, vmem),
        scratch_shapes=[
            pltpu.VMEM((ROWS, D), BF16),
            pltpu.VMEM((1, D), F32),
            pltpu.VMEM((ROWS, D), BF16),
            pltpu.VMEM((D, 2 * HD), BF16),
            pltpu.VMEM((HD, D), BF16),
            pltpu.VMEM((D, 2 * HD), BF16),
            pltpu.VMEM((8, 16, 2048), BF16),
            pltpu.VMEM((4, KVH, 2, 16, HD), BF16),
            pltpu.VMEM((2, 64, 2, 16, HD), BF16),
            pltpu.VMEM((ROWS, HD), BF16),
            pltpu.VMEM((4, ROWS, HD), BF16),
            pltpu.VMEM((2, 256, HD), BF16),
            pltpu.VMEM((2 * ROWS, HD), BF16),
            pltpu.VMEM((9, 2 * ROWS, 256), F32),
            pltpu.VMEM((2 * ROWS, 128), F32),
            pltpu.VMEM((2, 16, ROWS, 2 * HD), BF16),
            pltpu.VMEM((ROWS, 2 * HD), F32),
            pltpu.VMEM((4, 2 * RCH, HD), BF16),
            pltpu.VMEM((2, 2 * RCH, HD), BF16),
            pltpu.VMEM((2, KVH, 2, 2 * RCH, HD), BF16),
            sem((17,)),
            sem((1,)),
            sem((4,)),
            sem((1,)),
            sem((4,)),
            sem((2,)),
            sem((2,)),
            sem((1,)),
            sem((2,)),
            sem((2,)),
            sem((2,)),
            sem((1,)),
            sem((16,)),
            sem((1,)),
            sem((16,)),
        ],
        compiler_params=pltpu.CompilerParams(
            collective_id=0, has_side_effects=True, vmem_limit_bytes=56 * 1024 * 1024
        ),
        name="joined_attention",
    )(
        rows_in,
        norm_gain.reshape(1, D),
        w_query,
        w_keyval.T,
        w_out,
        page_pool,
        stretch_ids,
        page_slot,
        picked,
        question_len,
    )
    return pl.pallas_call(
        finish,
        out_shape=(
            jax.ShapeDtypeStruct(attn.shape, BF16),
            jax.ShapeDtypeStruct(joined.shape, BF16),
        ),
        in_specs=[vmem, vmem],
        out_specs=(any_spec, any_spec),
        scratch_shapes=[sem((2,))],
        name="write_out",
    )(pltpu.with_memory_space_constraint(attn, pltpu.VMEM), pltpu.with_memory_space_constraint(joined, pltpu.VMEM))


def solution(mesh):
    in_specs = (
        P("req", None, None),
        P(),
        P(None, "grp"),
        P(None, "grp"),
        P(None, "grp"),
        P("req", "grp", None),
        P(),
        P(),
        P(),
        P(),
    )
    out_specs = (P("req", None, "grp"), P("req", "grp", None))
    return jax.shard_map(local, mesh=mesh, in_specs=in_specs, out_specs=out_specs, check_vma=False)
```

```python
import functools
import math

import jax
import jax.numpy as jnp
from jax import lax
from jax.experimental import pallas as pl
from jax.experimental.pallas import tpu as pltpu
from jax.sharding import PartitionSpec as P

MESH = pl.DeviceIdType.MESH
F32 = jnp.float32
BF16 = jnp.bfloat16
HD = 128
KVH = 8
ROWS = 160
RCH = 24
SPANS = 4
D = 8192
KEYS = 2048
EPS = 1e-05
EXP2_SCALE = math.log2(math.e) / math.sqrt(HD)
NEG = -1e30
FAR = 1e9
LINE = (0, 1, 3, 2)
HOPS = (0, 1, 2, 1)
FARTHEST_FIRST = sorted(
    [(n // 16, n // 4 % 4, n % 4) for n in range(1, 64)], key=lambda steps: -sum(HOPS[d] for d in steps)
)


def nt_dot(a, b):
    return lax.dot_general(a, b, (((1,), (1,)), ((), ())), preferred_element_type=F32)


def nn_dot(a, b):
    return jnp.dot(a, b, preferred_element_type=F32)


def by_index(index, values):
    low = jnp.where(index == 0, values[0], values[1])
    return jnp.where(index < 2, low, jnp.where(index == 2, values[2], values[3]))


def to_column(row):
    n = row.shape[1]
    eye = lax.broadcasted_iota(jnp.int32, (n, n), 0) == lax.broadcasted_iota(jnp.int32, (n, n), 1)
    return jnp.sum(jnp.where(eye, jnp.broadcast_to(row, (n, n)), 0.0), axis=1, keepdims=True)


def kernel(
    rows_hbm,
    gain_hbm,
    wq_hbm,
    wk_hbm,
    wo_hbm,
    pool_hbm,
    ids_hbm,
    slots_hbm,
    picked_hbm,
    qlen_hbm,
    out_ref,
    joined_v,
    ids,
    slots,
    picked,
    qlen,
    rows_v,
    gain_v,
    nrm,
    wq_v,
    wk_v,
    wo_v,
    pool_v,
    sx,
    kv,
    kvp,
    fr,
    fk,
    q2,
    scores,
    peak,
    gath,
    acc,
    sj,
    rj1,
    rj,
    ld,
    zs_s,
    zs_r,
    cs_s,
    cs_r,
    fr_s,
    fr_r,
    js_s,
    js_r,
    jz_s,
    jz_r,
    g_s,
    g_r,
    gc_s,
    gc_r,
):
    r = lax.axis_index("req")
    m = lax.axis_index("grp")
    z = lax.div(m, 8)
    y = lax.rem(lax.div(m, 2), 4)
    c = lax.rem(m, 2)
    chip = lax.div(m, 2)
    k = lax.div(m, 4)
    sib = (r, m + 1 - 2 * c)

    def load(src, dst, i):
        cp = pltpu.make_async_copy(src, dst, ld.at[i])
        cp.start()
        return cp

    def push(src, dst, send, recv, dev):
        pltpu.make_async_remote_copy(
            src_ref=src, dst_ref=dst, send_sem=send, recv_sem=recv, device_id=dev, device_id_type=MESH
        ).start()

    def wait_all(ref, sem):
        pltpu.make_async_copy(ref, ref, sem).wait()

    barrier = pltpu.get_barrier_semaphore()

    def others(act, first=0, last=63):
        for dx, dy, dz in FARTHEST_FIRST[first:last]:
            act(lax.rem(r + dx, 4), 4 * lax.rem(z + dz, 4) + lax.rem(y + dy, 4))

    def greet(q, t):
        pl.semaphore_signal(barrier, inc=1, device_id=(q, 2 * t + c), device_id_type=MESH)

    others(greet)
    pl.semaphore_signal(barrier, inc=1, device_id=sib, device_id_type=MESH)

    ld_small = [
        load(ids_hbm, ids, 17),
        load(slots_hbm, slots, 18),
        load(qlen_hbm, qlen, 19),
        load(picked_hbm, picked, 20),
    ]
    for i in range(5):
        load(rows_hbm.at[0, pl.ds(32 * i, 32)], rows_v.at[pl.ds(32 * i, 32)], 1 + i)
    ld_gain = load(gain_hbm, gain_v, 6)
    ld_pool = load(pool_hbm, pool_v, 0)
    ld_wk = load(wk_hbm, wk_v.at[pl.ds(pl.multiple_of(64 * c, 64), 64)], 7)

    wk_v[pl.ds(pl.multiple_of(64 - 64 * c, 64), 64), :] = jnp.zeros((64, D), BF16)

    for cp in ld_small:
        cp.wait()
    place = [[slots[ids[q, s]] for s in range(SPANS)] for q in range(4)]
    send_slot, send_span = [], []
    for q in range(4):
        slot_q, span_q = 0, 0
        for s in range(SPANS):
            here = (place[q][s] >> 3) == r
            slot_q = slot_q + jnp.where(here, place[q][s] & 7, 0)
            span_q = span_q + jnp.where(here, s, 0)
        send_slot.append(slot_q)
        send_span.append(span_q)
    own_place = [slots[ids[r, s]] for s in range(SPANS)]
    span_of = []
    for x in range(4):
        span_x = 0
        for s in range(SPANS):
            span_x = span_x + jnp.where((own_place[s] >> 3) == x, s, 0)
        span_of.append(span_x)

    ld_pool.wait()
    row = lax.broadcasted_iota(jnp.int32, (64, 128), 0)
    wanted = by_index(row >> 4, send_slot) * 16 + (row & 15)
    pick_page = jnp.where(lax.broadcasted_iota(jnp.int32, (64, 128), 1) == wanted, 1.0, 0.0).astype(BF16)
    for h in range(2 * KVH):
        piece = nn_dot(pick_page, pool_v[:, :, h * HD : (h + 1) * HD].reshape(128, HD)).astype(BF16)
        for q in range(4):
            sx[q, h % KVH, h // KVH] = piece[16 * q : 16 * (q + 1)]
    ld_gain.wait()

    def norm(i, carry):
        at = pl.ds(pl.multiple_of(32 * i, 32), 32)
        wait_all(rows_v.at[at], ld.at[1 + i])
        squares = jnp.zeros((32, 128), F32)
        for j in range(D // 128):
            v = rows_v[at, j * 128 : (j + 1) * 128].astype(F32)
            squares = squares + v * v
        mean = jnp.sum(squares, axis=1, keepdims=True) * (1.0 / D)
        inv = jnp.broadcast_to(lax.rsqrt(mean + EPS), (32, 128))
        for j in range(D // 128):
            v = rows_v[at, j * 128 : (j + 1) * 128].astype(F32)
            nrm[at, j * 128 : (j + 1) * 128] = (v * inv * gain_v[:, j * 128 : (j + 1) * 128]).astype(BF16)
        return carry

    lax.fori_loop(0, 5, norm, 0)

    ld_wq = [
        load(wq_hbm.at[pl.ds(1024 * i, 1024)], wq_v.at[pl.ds(1024 * i, 1024)], 8 + i) for i in range(8)
    ]

    ld_wk.wait()
    new_kv = jnp.zeros((ROWS, HD), F32)
    for i in range(8):
        cols = slice(1024 * i, 1024 * (i + 1))
        new_kv = new_kv + nt_dot(nrm[:, cols], wk_v[:, cols])
    kvp[...] = new_kv.astype(BF16)
    pl.semaphore_wait(barrier, 64)
    head_to = lax.div(lax.rem(m, 16), 2)
    fr_slot = 2 * c + lax.div(m, 16)
    for i in range(2):
        t = 2 * head_to + i

        @pl.when(t == chip)
        def _():
            pltpu.make_async_copy(kvp, fr.at[fr_slot], fr_r.at[0]).start()

        @pl.when(t != chip)
        def _():
            push(kvp, fr.at[fr_slot], fr_s.at[0], fr_r.at[0], (r, 2 * t + c))

    def send_page(q, t):
        push(sx.at[q, lax.div(t, 2)], kv.at[c, 16 * r + chip], zs_s.at[0], zs_r.at[r], (q, 2 * t + c))

    pltpu.make_async_copy(sx.at[r, k], kv.at[c, 16 * r + chip], zs_r.at[r]).start()

    pl.when(m >= 0)(functools.partial(others, send_page))
    query = jnp.zeros((ROWS, 2 * HD), F32)
    for i in range(8):
        ld_wq[i].wait()
        at = slice(1024 * i, 1024 * (i + 1))
        query = query + nn_dot(nrm[:, at], wq_v[at, :])
    q2[0:ROWS, :] = query[:, 0:HD].astype(BF16)
    q2[ROWS : 2 * ROWS, :] = query[:, HD : 2 * HD].astype(BF16)

    own_half = fr.at[pl.ds(2 * c, 2)]
    wait_all(own_half, fr_r.at[0])
    push(own_half, own_half, fr_s.at[1], fr_r.at[1], sib)
    ld_wo = load(wo_hbm, wo_v, 16)

    own_picked = picked[r].astype(F32)
    cols = [to_column(own_picked[s : s + 1, :]) + 512.0 * s for s in range(SPANS)]
    question = lax.broadcasted_iota(jnp.int32, (64, 1), 0).astype(F32)
    own_len = qlen[r].astype(F32)
    row_pos = jnp.concatenate(cols + [question + float(KEYS)], axis=0)
    key_col = jnp.concatenate(cols + [jnp.where(question < own_len, question + float(KEYS), FAR)], axis=0)
    eye = lax.broadcasted_iota(jnp.int32, (ROWS, 256), 0) == lax.broadcasted_iota(jnp.int32, (ROWS, 256), 1)
    fresh_pos = jnp.sum(jnp.where(eye, jnp.broadcast_to(key_col, (ROWS, 256)), 0.0), axis=0, keepdims=True)
    fresh_pos = jnp.where(lax.broadcasted_iota(jnp.int32, (1, 256), 1) < ROWS, fresh_pos, FAR)
    row_pos_b = jnp.broadcast_to(row_pos, (ROWS, 256))
    picked_b = row_pos_b[0 : SPANS * RCH]

    wait_all(fr.at[pl.ds(2 - 2 * c, 2)], fr_r.at[1])
    row = lax.broadcasted_iota(jnp.int32, (SPANS * RCH, 256), 0)
    wanted = by_index(lax.div(row, RCH), span_of) * RCH + lax.rem(row, RCH)
    pick_rows = jnp.where(lax.broadcasted_iota(jnp.int32, (SPANS * RCH, 256), 1) == wanted, 1.0, 0.0).astype(BF16)
    by_holder = []
    for s in range(2):
        fk[s, 0:ROWS, :] = (fr[s].astype(F32) + fr[2 + s].astype(F32)).astype(BF16)
        fk[s, ROWS:256, :] = jnp.zeros((256 - ROWS, HD), BF16)
        by_holder.append(nn_dot(pick_rows, fk[s]))
    for x in range(4):
        sj[x] = jnp.concatenate([b[x * RCH : (x + 1) * RCH] for b in by_holder], axis=0).astype(BF16)
    rj_half = lax.div(r, 2)
    rj_slot = lax.rem(r, 2)

    @pl.when(rj_half == c)
    def _():
        for d in (2, 1, 3):
            x = lax.rem(r + d, 4)
            push(sj.at[x], rj1.at[rj_slot], js_s.at[0], js_r.at[rj_slot], (x, m))
        rj1[rj_slot] = sj[r]

    def score(at, keys, key_pos):
        s = nt_dot(q2[...], keys)
        seen = row_pos_b >= jnp.broadcast_to(key_pos, (ROWS, 256))
        for half in range(2):
            rows = slice(half * ROWS, (half + 1) * ROWS)
            masked = jnp.where(seen, s[rows], NEG)
            scores[at, rows, :] = masked
            peak[rows, :] = jnp.maximum(peak[rows, :], jnp.maximum(masked[:, :128], masked[:, 128:]))

    peak[...] = jnp.full((2 * ROWS, 128), NEG, F32)
    score(8, fk[0], fresh_pos)

    def group(cc, x):
        return kv.at[cc, pl.ds(16 * x, 16)]

    for d in (2, 1, 3, 0):
        x = lax.rem(r + d, 4)
        wait_all(group(c, x), zs_r.at[x])
        push(group(c, x), group(c, x), cs_s.at[0], cs_r.at[x], sib)

    for q in range(2):

        @pl.when(r != 2 * c + q)
        def _():
            wait_all(rj1.at[q], js_r.at[q])

    rj[c, k] = rj1[...]

    def spread_fresh(d, carry):
        t = lax.rem(k + d, 8)
        push(rj1, rj.at[c, k], jz_s.at[0], jz_r.at[0], (r, (2 * t + lax.rem(y, 2)) * 2 + c))
        return carry

    lax.fori_loop(1, 8, spread_fresh, 0)

    lane = lax.broadcasted_iota(jnp.int32, (1, 256), 1)
    lane_pos = (lane >> 4) * 32 + (lane & 15)

    def page_keys(cc, x):
        span = jnp.where(x == 0, span_of[0], jnp.where(x == 1, span_of[1], jnp.where(x == 2, span_of[2], span_of[3])))
        pos = (lane_pos + (span * 512 + cc * 16)).astype(F32)
        same = picked_b == jnp.broadcast_to(pos, (SPANS * RCH, 256))
        gone = jnp.max(jnp.where(same, 1.0, 0.0), axis=0, keepdims=True)
        return jnp.where(gone > 0.5, FAR, pos)

    def page_part(cc, x, s):
        return kv[cc, pl.ds(16 * x, 16), s].reshape(256, HD)

    for x in range(4):
        score(4 * c + x, page_part(c, x, 0), page_keys(c, x))

    for x in range(4):
        wait_all(group(1 - c, x), cs_r.at[x])
        score(4 * (1 - c) + x, page_part(1 - c, x, 0), page_keys(1 - c, x))

    for h in range(2):
        rows = slice(h * ROWS, (h + 1) * ROWS)
        top = jnp.broadcast_to(jnp.max(peak[rows, :], axis=1, keepdims=True), (ROWS, 128))
        total = jnp.zeros((ROWS, 128), F32)
        mixed = jnp.zeros((ROWS, HD), F32)
        for i in range(9):
            w0 = jnp.exp2((scores[i, rows, 0:128] - top) * EXP2_SCALE)
            w1 = jnp.exp2((scores[i, rows, 128:256] - top) * EXP2_SCALE)
            total = total + (w0 + w1)
            vals = fk[1] if i == 8 else page_part(i // 4, i % 4, 1)
            mixed = mixed + nn_dot(jnp.concatenate([w0, w1], axis=1).astype(BF16), vals)
        att = mixed / jnp.sum(total, axis=1, keepdims=True)
        gath[c, chip, :, h * HD : (h + 1) * HD] = att.astype(BF16)

    def chip_at(cc, df, ds):
        f = lax.rem(y * (1 - cc) + z * cc + df, 4)
        s = lax.rem(z * (1 - cc) + y * cc + ds, 4)
        return (4 * s + f) * (1 - cc) + (4 * f + s) * cc

    def forward(block, df, ds):
        ref = gath.at[c, block]
        push(ref, ref, g_s.at[0], g_r.at[block], (r, 2 * chip_at(c, df, ds) + c))

    def across(block):
        ref = gath.at[c, block]
        push(ref, ref, gc_s.at[0], gc_r.at[block], sib)

    def arrived(block):
        wait_all(gath.at[c, block], g_r.at[block])

    def project(cc, ds):
        more = jnp.zeros((ROWS, 2 * HD), F32)
        for df in LINE:
            block = chip_at(cc, df, ds)
            at = pl.multiple_of((2 * block + cc) * 256, 256)
            more = more + nn_dot(gath[cc, block], wo_v[pl.ds(at, 256), :])
        acc[...] += more

    def crossed(ds):
        for df in LINE:
            block = chip_at(1 - c, df, ds)
            wait_all(gath.at[1 - c, block], gc_r.at[block])

    for df in (1, 3, 2):
        forward(chip, df, 0)
    across(chip)
    for ds in (1, 3):
        forward(chip, 0, ds)
    acc[...] = jnp.zeros((ROWS, 2 * HD), F32)
    for df in (1, 3, 2):
        block = chip_at(c, df, 0)
        arrived(block)
        for ds in (2, 1, 3) if df == 2 else (1, 3):
            forward(block, 0, ds)
        across(block)
        if df == 3:
            forward(chip, 0, 2)
    ld_wo.wait()
    project(c, 0)
    for df, ds in ((0, 1), (0, 3), (1, 3), (3, 1), (1, 1), (3, 3), (2, 1), (2, 3), (0, 2)):
        block = chip_at(c, df, ds)
        arrived(block)
        if (df, ds) in ((1, 3), (3, 1)):
            forward(block, 0, 4 - ds)
        across(block)
    crossed(0)
    wait_all(rj.at[c, pl.ds(0, 7)], jz_r.at[0])
    push(rj.at[c], rj.at[c], jz_s.at[1], jz_r.at[1], sib)
    project(1 - c, 0)
    project(c, 1)
    project(c, 3)

    crossed(1)
    project(1 - c, 1)
    crossed(3)
    project(1 - c, 3)
    for df in (2, 1, 3):
        block = chip_at(c, df, 2)
        arrived(block)
        across(block)
    project(c, 2)
    wait_all(rj.at[1 - c], jz_r.at[1])
    col = lax.broadcasted_iota(jnp.int32, (RCH, 192), 1)
    col_req = lax.div(col, 48)
    col_in = lax.rem(col, 48)
    row_in = lax.broadcasted_iota(jnp.int32, (RCH, 192), 0)
    target = jnp.zeros((1, 192), F32)
    low = (m * 16).astype(F32)
    for q in range(4):
        pq = picked[q].astype(F32)
        mine = jnp.zeros((1, RCH), F32)
        for s in range(SPANS):
            mine = mine + jnp.where(send_span[q] == s, pq[s : s + 1, :], 0.0)
        mine = mine - low
        mine = jnp.where((mine >= 0.0) & (mine < 16.0), mine + (send_slot[q] * 16).astype(F32), -1.0)
        fits = (col_req == q) & ((col_in == row_in) | (col_in == row_in + RCH))
        target = target + jnp.sum(
            jnp.where(fits, jnp.broadcast_to(to_column(mine), (RCH, 192)), 0.0), axis=0, keepdims=True
        )
    line = lax.broadcasted_iota(jnp.int32, (128, 192), 0).astype(F32)
    is_key = lax.rem(lax.broadcasted_iota(jnp.int32, (128, 192), 1), 48) < RCH
    match = line == jnp.broadcast_to(target, (128, 192))
    pick_key = jnp.where(match & is_key, 1.0, 0.0)
    pick_val = jnp.where(match & jnp.logical_not(is_key), 1.0, 0.0)
    hit = jnp.broadcast_to(jnp.max(pick_key, axis=1, keepdims=True), (128, HD)) > 0.5
    pick = jnp.concatenate([pick_key, pick_val], axis=0).astype(BF16)
    for h in range(KVH):
        new = nn_dot(pick[:, 0:96], rj[0, h].reshape(96, HD)) + nn_dot(pick[:, 96:192], rj[1, h].reshape(96, HD))
        for s in range(2):
            at = slice(1024 * s + h * HD, 1024 * s + (h + 1) * HD)
            old = pool_v[:, :, at].astype(F32).reshape(128, HD)
            joined_v[:, :, at] = (
                jnp.where(hit, new[128 * s : 128 * (s + 1)], old).astype(BF16).reshape(8, 16, HD)
            )

    crossed(2)
    project(1 - c, 2)
    live = lax.broadcasted_iota(jnp.int32, (ROWS, 2 * HD), 0) < SPANS * RCH + qlen[r]
    out_ref[0] = jnp.where(live, acc[...], 0.0).astype(BF16)

    wait_all(kv.at[0, pl.ds(0, 63)], zs_s.at[0])
    wait_all(kv.at[0], cs_s.at[0])

    wait_all(own_half, fr_s.at[1])

    @pl.when(head_to == k)
    def _():
        wait_all(fr.at[pl.ds(0, 1)], fr_s.at[0])

    @pl.when(head_to != k)
    def _():
        wait_all(fr.at[pl.ds(0, 2)], fr_s.at[0])


    @pl.when(rj_half == c)
    def _():
        wait_all(sj.at[pl.ds(0, 3)], js_s.at[0])

    wait_all(rj.at[0, pl.ds(0, 7)], jz_s.at[0])
    wait_all(rj.at[0], jz_s.at[1])
    wait_all(gath.at[0, pl.ds(0, 15)], g_s.at[0])
    wait_all(gath.at[0], gc_s.at[0])


def finish(attn, joined, attn_out, joined_out, sems):
    copies = [
        pltpu.make_async_copy(joined, joined_out, sems.at[0]),
        pltpu.make_async_copy(attn, attn_out, sems.at[1]),
    ]
    for cp in copies:
        cp.start()
    for cp in copies:
        cp.wait()


def local(
    rows_in, norm_gain, w_query, w_keyval, w_out, page_pool, stretch_ids, page_slot, picked, question_len
):
    any_spec = pl.BlockSpec(memory_space=pl.ANY)
    vmem = pl.BlockSpec(memory_space=pltpu.VMEM)
    sem = pltpu.SemaphoreType.DMA
    attn, joined = pl.pallas_call(
        kernel,
        out_shape=(pltpu.VMEM((1, ROWS, 2 * HD), BF16), pltpu.VMEM(page_pool.shape, BF16)),
        in_specs=[any_spec] * 10,
        out_specs=(vmem, vmem),
        scratch_shapes=[
            pltpu.SMEM((4, SPANS), jnp.int32),
            pltpu.SMEM((32,), jnp.int32),
            pltpu.VMEM((4, SPANS, RCH), jnp.int32),
            pltpu.SMEM((4,), jnp.int32),
            pltpu.VMEM((ROWS, D), BF16),
            pltpu.VMEM((1, D), F32),
            pltpu.VMEM((ROWS, D), BF16),
            pltpu.VMEM((D, 2 * HD), BF16),
            pltpu.VMEM((HD, D), BF16),
            pltpu.VMEM((D, 2 * HD), BF16),
            pltpu.VMEM((8, 16, 2048), BF16),
            pltpu.VMEM((4, KVH, 2, 16, HD), BF16),
            pltpu.VMEM((2, 64, 2, 16, HD), BF16),
            pltpu.VMEM((ROWS, HD), BF16),
            pltpu.VMEM((4, ROWS, HD), BF16),
            pltpu.VMEM((2, 256, HD), BF16),
            pltpu.VMEM((2 * ROWS, HD), BF16),
            pltpu.VMEM((9, 2 * ROWS, 256), F32),
            pltpu.VMEM((2 * ROWS, 128), F32),
            pltpu.VMEM((2, 16, ROWS, 2 * HD), BF16),
            pltpu.VMEM((ROWS, 2 * HD), F32),
            pltpu.VMEM((4, 2 * RCH, HD), BF16),
            pltpu.VMEM((2, 2 * RCH, HD), BF16),
            pltpu.VMEM((2, KVH, 2, 2 * RCH, HD), BF16),
            sem((21,)),
            sem((1,)),
            sem((4,)),
            sem((1,)),
            sem((4,)),
            sem((2,)),
            sem((2,)),
            sem((1,)),
            sem((2,)),
            sem((2,)),
            sem((2,)),
            sem((1,)),
            sem((16,)),
            sem((1,)),
            sem((16,)),
        ],
        compiler_params=pltpu.CompilerParams(
            collective_id=0, has_side_effects=True, vmem_limit_bytes=56 * 1024 * 1024
        ),
        name="joined_attention",
    )(
        rows_in,
        norm_gain.reshape(1, D),
        w_query,
        w_keyval.T,
        w_out,
        page_pool,
        stretch_ids,
        page_slot,
        picked,
        question_len,
    )
    return pl.pallas_call(
        finish,
        out_shape=(
            jax.ShapeDtypeStruct(attn.shape, BF16),
            jax.ShapeDtypeStruct(joined.shape, BF16),
        ),
        in_specs=[vmem, vmem],
        out_specs=(any_spec, any_spec),
        scratch_shapes=[sem((2,))],
        name="write_out",
    )(pltpu.with_memory_space_constraint(attn, pltpu.VMEM), pltpu.with_memory_space_constraint(joined, pltpu.VMEM))


def solution(mesh):
    in_specs = (
        P("req", None, None),
        P(),
        P(None, "grp"),
        P(None, "grp"),
        P(None, "grp"),
        P("req", "grp", None),
        P(),
        P(),
        P(),
        P(),
    )
    out_specs = (P("req", None, "grp"), P("req", "grp", None))
    return jax.shard_map(local, mesh=mesh, in_specs=in_specs, out_specs=out_specs, check_vma=False)
```

```python
import functools
import math

import jax
import jax.numpy as jnp
from jax import lax
from jax.experimental import pallas as pl
from jax.experimental.pallas import tpu as pltpu
from jax.sharding import PartitionSpec as P

MESH = pl.DeviceIdType.MESH
F32 = jnp.float32
BF16 = jnp.bfloat16
HD = 128
KVH = 8
ROWS = 160
RCH = 24
SPANS = 4
D = 8192
KEYS = 2048
EPS = 1e-05
EXP2_SCALE = math.log2(math.e) / math.sqrt(HD)
NEG = -1e30
FAR = 1e9
LINE = (0, 1, 3, 2)
HOPS = (0, 1, 2, 1)
FARTHEST_FIRST = sorted(
    [(n // 16, n // 4 % 4, n % 4) for n in range(1, 64)], key=lambda steps: -sum(HOPS[d] for d in steps)
)


def nt_dot(a, b):
    return lax.dot_general(a, b, (((1,), (1,)), ((), ())), preferred_element_type=F32)


def nn_dot(a, b):
    return jnp.dot(a, b, preferred_element_type=F32)


def by_index(index, values):
    low = jnp.where(index == 0, values[0], values[1])
    return jnp.where(index < 2, low, jnp.where(index == 2, values[2], values[3]))


def to_column(row):
    n = row.shape[1]
    eye = lax.broadcasted_iota(jnp.int32, (n, n), 0) == lax.broadcasted_iota(jnp.int32, (n, n), 1)
    return jnp.sum(jnp.where(eye, jnp.broadcast_to(row, (n, n)), 0.0), axis=1, keepdims=True)


def kernel(
    rows_hbm,
    gain_hbm,
    wq_hbm,
    wk_hbm,
    wo_hbm,
    pool_hbm,
    ids_hbm,
    slots_hbm,
    picked_hbm,
    qlen_hbm,
    out_ref,
    joined_v,
    ids,
    slots,
    picked,
    qlen,
    rows_v,
    gain_v,
    nrm,
    wq_v,
    wk_v,
    wo_v,
    pool_v,
    sx,
    kv,
    kvp,
    fr,
    fk,
    q2,
    scores,
    peak,
    gath,
    acc,
    sj,
    rj1,
    rj,
    ld,
    zs_s,
    zs_r,
    cs_s,
    cs_r,
    fr_s,
    fr_r,
    js_s,
    js_r,
    jz_s,
    jz_r,
    g_s,
    g_r,
    gc_s,
    gc_r,
):
    r = lax.axis_index("req")
    m = lax.axis_index("grp")
    z = lax.div(m, 8)
    y = lax.rem(lax.div(m, 2), 4)
    c = lax.rem(m, 2)
    chip = lax.div(m, 2)
    k = lax.div(m, 4)
    sib = (r, m + 1 - 2 * c)

    def load(src, dst, i):
        cp = pltpu.make_async_copy(src, dst, ld.at[i])
        cp.start()
        return cp

    def push(src, dst, send, recv, dev):
        pltpu.make_async_remote_copy(
            src_ref=src, dst_ref=dst, send_sem=send, recv_sem=recv, device_id=dev, device_id_type=MESH
        ).start()

    def wait_all(ref, sem):
        pltpu.make_async_copy(ref, ref, sem).wait()

    barrier = pltpu.get_barrier_semaphore()

    def others(act, first=0, last=63):
        for dx, dy, dz in FARTHEST_FIRST[first:last]:
            act(lax.rem(r + dx, 4), 4 * lax.rem(z + dz, 4) + lax.rem(y + dy, 4))

    def greet(q, t):
        pl.semaphore_signal(barrier, inc=1, device_id=(q, 2 * t + c), device_id_type=MESH)

    others(greet)
    pl.semaphore_signal(barrier, inc=1, device_id=sib, device_id_type=MESH)

    ld_small = [
        load(ids_hbm, ids, 17),
        load(slots_hbm, slots, 18),
        load(qlen_hbm, qlen, 19),
        load(picked_hbm, picked, 20),
    ]
    for i in range(5):
        load(rows_hbm.at[0, pl.ds(32 * i, 32)], rows_v.at[pl.ds(32 * i, 32)], 1 + i)
    ld_gain = load(gain_hbm, gain_v, 6)
    ld_pool = load(pool_hbm, pool_v, 0)
    ld_wk = load(wk_hbm, wk_v.at[pl.ds(pl.multiple_of(64 * c, 64), 64)], 7)
    ld_wq = [
        load(wq_hbm.at[pl.ds(1024 * i, 1024)], wq_v.at[pl.ds(1024 * i, 1024)], 8 + i) for i in range(8)
    ]

    wk_v[pl.ds(pl.multiple_of(64 - 64 * c, 64), 64), :] = jnp.zeros((64, D), BF16)

    for cp in ld_small:
        cp.wait()
    place = [[slots[ids[q, s]] for s in range(SPANS)] for q in range(4)]
    send_slot, send_span = [], []
    for q in range(4):
        slot_q, span_q = 0, 0
        for s in range(SPANS):
            here = (place[q][s] >> 3) == r
            slot_q = slot_q + jnp.where(here, place[q][s] & 7, 0)
            span_q = span_q + jnp.where(here, s, 0)
        send_slot.append(slot_q)
        send_span.append(span_q)
    own_place = [slots[ids[r, s]] for s in range(SPANS)]
    span_of = []
    for x in range(4):
        span_x = 0
        for s in range(SPANS):
            span_x = span_x + jnp.where((own_place[s] >> 3) == x, s, 0)
        span_of.append(span_x)

    ld_pool.wait()
    row = lax.broadcasted_iota(jnp.int32, (64, 128), 0)
    wanted = by_index(row >> 4, send_slot) * 16 + (row & 15)
    pick_page = jnp.where(lax.broadcasted_iota(jnp.int32, (64, 128), 1) == wanted, 1.0, 0.0).astype(BF16)
    for h in range(2 * KVH):
        piece = nn_dot(pick_page, pool_v[:, :, h * HD : (h + 1) * HD].reshape(128, HD)).astype(BF16)
        for q in range(4):
            sx[q, h % KVH, h // KVH] = piece[16 * q : 16 * (q + 1)]
    ld_gain.wait()

    def norm(i, carry):
        at = pl.ds(pl.multiple_of(32 * i, 32), 32)
        wait_all(rows_v.at[at], ld.at[1 + i])
        squares = jnp.zeros((32, 128), F32)
        for j in range(D // 128):
            v = rows_v[at, j * 128 : (j + 1) * 128].astype(F32)
            squares = squares + v * v
        mean = jnp.sum(squares, axis=1, keepdims=True) * (1.0 / D)
        inv = jnp.broadcast_to(lax.rsqrt(mean + EPS), (32, 128))
        for j in range(D // 128):
            v = rows_v[at, j * 128 : (j + 1) * 128].astype(F32)
            nrm[at, j * 128 : (j + 1) * 128] = (v * inv * gain_v[:, j * 128 : (j + 1) * 128]).astype(BF16)
        return carry

    lax.fori_loop(0, 5, norm, 0)


    ld_wk.wait()
    new_kv = jnp.zeros((ROWS, HD), F32)
    for i in range(8):
        cols = slice(1024 * i, 1024 * (i + 1))
        new_kv = new_kv + nt_dot(nrm[:, cols], wk_v[:, cols])
    kvp[...] = new_kv.astype(BF16)
    pl.semaphore_wait(barrier, 64)
    head_to = lax.div(lax.rem(m, 16), 2)
    fr_slot = 2 * c + lax.div(m, 16)
    for i in range(2):
        t = 2 * head_to + i

        @pl.when(t == chip)
        def _():
            pltpu.make_async_copy(kvp, fr.at[fr_slot], fr_r.at[0]).start()

        @pl.when(t != chip)
        def _():
            push(kvp, fr.at[fr_slot], fr_s.at[0], fr_r.at[0], (r, 2 * t + c))

    def send_page(q, t):
        push(sx.at[q, lax.div(t, 2)], kv.at[c, 16 * r + chip], zs_s.at[0], zs_r.at[r], (q, 2 * t + c))

    pltpu.make_async_copy(sx.at[r, k], kv.at[c, 16 * r + chip], zs_r.at[r]).start()

    pl.when(m >= 0)(functools.partial(others, send_page))
    query = jnp.zeros((ROWS, 2 * HD), F32)
    for i in range(8):
        ld_wq[i].wait()
        at = slice(1024 * i, 1024 * (i + 1))
        query = query + nn_dot(nrm[:, at], wq_v[at, :])
    q2[0:ROWS, :] = query[:, 0:HD].astype(BF16)
    q2[ROWS : 2 * ROWS, :] = query[:, HD : 2 * HD].astype(BF16)

    own_half = fr.at[pl.ds(2 * c, 2)]
    wait_all(own_half, fr_r.at[0])
    push(own_half, own_half, fr_s.at[1], fr_r.at[1], sib)

    own_picked = picked[r].astype(F32)
    cols = [to_column(own_picked[s : s + 1, :]) + 512.0 * s for s in range(SPANS)]
    question = lax.broadcasted_iota(jnp.int32, (64, 1), 0).astype(F32)
    own_len = qlen[r].astype(F32)
    row_pos = jnp.concatenate(cols + [question + float(KEYS)], axis=0)
    key_col = jnp.concatenate(cols + [jnp.where(question < own_len, question + float(KEYS), FAR)], axis=0)
    eye = lax.broadcasted_iota(jnp.int32, (ROWS, 256), 0) == lax.broadcasted_iota(jnp.int32, (ROWS, 256), 1)
    fresh_pos = jnp.sum(jnp.where(eye, jnp.broadcast_to(key_col, (ROWS, 256)), 0.0), axis=0, keepdims=True)
    fresh_pos = jnp.where(lax.broadcasted_iota(jnp.int32, (1, 256), 1) < ROWS, fresh_pos, FAR)
    row_pos_b = jnp.broadcast_to(row_pos, (ROWS, 256))
    picked_b = row_pos_b[0 : SPANS * RCH]

    wait_all(fr.at[pl.ds(2 - 2 * c, 2)], fr_r.at[1])
    row = lax.broadcasted_iota(jnp.int32, (SPANS * RCH, 256), 0)
    wanted = by_index(lax.div(row, RCH), span_of) * RCH + lax.rem(row, RCH)
    pick_rows = jnp.where(lax.broadcasted_iota(jnp.int32, (SPANS * RCH, 256), 1) == wanted, 1.0, 0.0).astype(BF16)
    by_holder = []
    for s in range(2):
        fk[s, 0:ROWS, :] = (fr[s].astype(F32) + fr[2 + s].astype(F32)).astype(BF16)
        fk[s, ROWS:256, :] = jnp.zeros((256 - ROWS, HD), BF16)
        by_holder.append(nn_dot(pick_rows, fk[s]))
    for x in range(4):
        sj[x] = jnp.concatenate([b[x * RCH : (x + 1) * RCH] for b in by_holder], axis=0).astype(BF16)
    rj_half = lax.div(r, 2)
    rj_slot = lax.rem(r, 2)

    @pl.when(rj_half == c)
    def _():
        for d in (2, 1, 3):
            x = lax.rem(r + d, 4)
            push(sj.at[x], rj1.at[rj_slot], js_s.at[0], js_r.at[rj_slot], (x, m))
        rj1[rj_slot] = sj[r]

    def score(at, keys, key_pos):
        s = nt_dot(q2[...], keys)
        seen = row_pos_b >= jnp.broadcast_to(key_pos, (ROWS, 256))
        for half in range(2):
            rows = slice(half * ROWS, (half + 1) * ROWS)
            masked = jnp.where(seen, s[rows], NEG)
            scores[at, rows, :] = masked
            peak[rows, :] = jnp.maximum(peak[rows, :], jnp.maximum(masked[:, :128], masked[:, 128:]))

    peak[...] = jnp.full((2 * ROWS, 128), NEG, F32)
    score(8, fk[0], fresh_pos)

    def group(cc, x):
        return kv.at[cc, pl.ds(16 * x, 16)]

    for d in (2, 1, 3, 0):
        x = lax.rem(r + d, 4)
        wait_all(group(c, x), zs_r.at[x])
        push(group(c, x), group(c, x), cs_s.at[0], cs_r.at[x], sib)

    for q in range(2):

        @pl.when(r != 2 * c + q)
        def _():
            wait_all(rj1.at[q], js_r.at[q])

    rj[c, k] = rj1[...]

    def spread_fresh(d, carry):
        t = lax.rem(k + d, 8)
        push(rj1, rj.at[c, k], jz_s.at[0], jz_r.at[0], (r, (2 * t + lax.rem(y, 2)) * 2 + c))
        return carry

    lax.fori_loop(1, 8, spread_fresh, 0)

    ld_wo = load(wo_hbm, wo_v, 16)
    lane = lax.broadcasted_iota(jnp.int32, (1, 256), 1)
    lane_pos = (lane >> 4) * 32 + (lane & 15)

    def page_keys(cc, x):
        span = jnp.where(x == 0, span_of[0], jnp.where(x == 1, span_of[1], jnp.where(x == 2, span_of[2], span_of[3])))
        pos = (lane_pos + (span * 512 + cc * 16)).astype(F32)
        same = picked_b == jnp.broadcast_to(pos, (SPANS * RCH, 256))
        gone = jnp.max(jnp.where(same, 1.0, 0.0), axis=0, keepdims=True)
        return jnp.where(gone > 0.5, FAR, pos)

    def page_part(cc, x, s):
        return kv[cc, pl.ds(16 * x, 16), s].reshape(256, HD)

    for x in range(4):
        score(4 * c + x, page_part(c, x, 0), page_keys(c, x))

    for x in range(4):
        wait_all(group(1 - c, x), cs_r.at[x])
        score(4 * (1 - c) + x, page_part(1 - c, x, 0), page_keys(1 - c, x))

    for h in range(2):
        rows = slice(h * ROWS, (h + 1) * ROWS)
        top = jnp.broadcast_to(jnp.max(peak[rows, :], axis=1, keepdims=True), (ROWS, 128))
        total = jnp.zeros((ROWS, 128), F32)
        mixed = jnp.zeros((ROWS, HD), F32)
        for i in range(9):
            w0 = jnp.exp2((scores[i, rows, 0:128] - top) * EXP2_SCALE)
            w1 = jnp.exp2((scores[i, rows, 128:256] - top) * EXP2_SCALE)
            total = total + (w0 + w1)
            vals = fk[1] if i == 8 else page_part(i // 4, i % 4, 1)
            mixed = mixed + nn_dot(jnp.concatenate([w0, w1], axis=1).astype(BF16), vals)
        att = mixed / jnp.sum(total, axis=1, keepdims=True)
        gath[c, chip, :, h * HD : (h + 1) * HD] = att.astype(BF16)

    def chip_at(cc, df, ds):
        f = lax.rem(y * (1 - cc) + z * cc + df, 4)
        s = lax.rem(z * (1 - cc) + y * cc + ds, 4)
        return (4 * s + f) * (1 - cc) + (4 * f + s) * cc

    def forward(block, df, ds):
        ref = gath.at[c, block]
        push(ref, ref, g_s.at[0], g_r.at[block], (r, 2 * chip_at(c, df, ds) + c))

    def across(block):
        ref = gath.at[c, block]
        push(ref, ref, gc_s.at[0], gc_r.at[block], sib)

    def arrived(block):
        wait_all(gath.at[c, block], g_r.at[block])

    def project(cc, ds):
        more = jnp.zeros((ROWS, 2 * HD), F32)
        for df in LINE:
            block = chip_at(cc, df, ds)
            at = pl.multiple_of((2 * block + cc) * 256, 256)
            more = more + nn_dot(gath[cc, block], wo_v[pl.ds(at, 256), :])
        acc[...] += more

    def crossed(ds):
        for df in LINE:
            block = chip_at(1 - c, df, ds)
            wait_all(gath.at[1 - c, block], gc_r.at[block])

    for df in (1, 3, 2):
        forward(chip, df, 0)
    across(chip)
    for ds in (1, 3):
        forward(chip, 0, ds)
    acc[...] = jnp.zeros((ROWS, 2 * HD), F32)
    for df in (1, 3, 2):
        block = chip_at(c, df, 0)
        arrived(block)
        for ds in (2, 1, 3) if df == 2 else (1, 3):
            forward(block, 0, ds)
        across(block)
    ld_wo.wait()
    project(c, 0)
    for df, ds in ((0, 1), (0, 3), (1, 3), (3, 1), (1, 1), (3, 3), (2, 1), (2, 3), (0, 2)):
        block = chip_at(c, df, ds)
        arrived(block)
        if (df, ds) in ((0, 1), (1, 3), (3, 1)):
            forward(block, 0, 4 - ds)
        across(block)
    crossed(0)
    wait_all(rj.at[c, pl.ds(0, 7)], jz_r.at[0])
    push(rj.at[c], rj.at[c], jz_s.at[1], jz_r.at[1], sib)
    project(1 - c, 0)
    project(c, 1)
    project(c, 3)

    crossed(1)
    project(1 - c, 1)
    crossed(3)
    project(1 - c, 3)
    for df in (2, 1, 3):
        block = chip_at(c, df, 2)
        arrived(block)
        across(block)
    project(c, 2)
    wait_all(rj.at[1 - c], jz_r.at[1])
    col = lax.broadcasted_iota(jnp.int32, (RCH, 192), 1)
    col_req = lax.div(col, 48)
    col_in = lax.rem(col, 48)
    row_in = lax.broadcasted_iota(jnp.int32, (RCH, 192), 0)
    target = jnp.zeros((1, 192), F32)
    low = (m * 16).astype(F32)
    for q in range(4):
        pq = picked[q].astype(F32)
        mine = jnp.zeros((1, RCH), F32)
        for s in range(SPANS):
            mine = mine + jnp.where(send_span[q] == s, pq[s : s + 1, :], 0.0)
        mine = mine - low
        mine = jnp.where((mine >= 0.0) & (mine < 16.0), mine + (send_slot[q] * 16).astype(F32), -1.0)
        fits = (col_req == q) & ((col_in == row_in) | (col_in == row_in + RCH))
        target = target + jnp.sum(
            jnp.where(fits, jnp.broadcast_to(to_column(mine), (RCH, 192)), 0.0), axis=0, keepdims=True
        )
    line = lax.broadcasted_iota(jnp.int32, (128, 192), 0).astype(F32)
    is_key = lax.rem(lax.broadcasted_iota(jnp.int32, (128, 192), 1), 48) < RCH
    match = line == jnp.broadcast_to(target, (128, 192))
    pick_key = jnp.where(match & is_key, 1.0, 0.0)
    pick_val = jnp.where(match & jnp.logical_not(is_key), 1.0, 0.0)
    hit = jnp.broadcast_to(jnp.max(pick_key, axis=1, keepdims=True), (128, HD)) > 0.5
    pick = jnp.concatenate([pick_key, pick_val], axis=0).astype(BF16)
    for h in range(KVH):
        new = nn_dot(pick[:, 0:96], rj[0, h].reshape(96, HD)) + nn_dot(pick[:, 96:192], rj[1, h].reshape(96, HD))
        for s in range(2):
            at = slice(1024 * s + h * HD, 1024 * s + (h + 1) * HD)
            old = pool_v[:, :, at].astype(F32).reshape(128, HD)
            joined_v[:, :, at] = (
                jnp.where(hit, new[128 * s : 128 * (s + 1)], old).astype(BF16).reshape(8, 16, HD)
            )

    crossed(2)
    project(1 - c, 2)
    live = lax.broadcasted_iota(jnp.int32, (ROWS, 2 * HD), 0) < SPANS * RCH + qlen[r]
    out_ref[0] = jnp.where(live, acc[...], 0.0).astype(BF16)

    wait_all(kv.at[0, pl.ds(0, 63)], zs_s.at[0])
    wait_all(kv.at[0], cs_s.at[0])

    wait_all(own_half, fr_s.at[1])

    @pl.when(head_to == k)
    def _():
        wait_all(fr.at[pl.ds(0, 1)], fr_s.at[0])

    @pl.when(head_to != k)
    def _():
        wait_all(fr.at[pl.ds(0, 2)], fr_s.at[0])


    @pl.when(rj_half == c)
    def _():
        wait_all(sj.at[pl.ds(0, 3)], js_s.at[0])

    wait_all(rj.at[0, pl.ds(0, 7)], jz_s.at[0])
    wait_all(rj.at[0], jz_s.at[1])
    wait_all(gath.at[0, pl.ds(0, 15)], g_s.at[0])
    wait_all(gath.at[0], gc_s.at[0])


def finish(attn, joined, attn_out, joined_out, sems):
    copies = [
        pltpu.make_async_copy(joined, joined_out, sems.at[0]),
        pltpu.make_async_copy(attn, attn_out, sems.at[1]),
    ]
    for cp in copies:
        cp.start()
    for cp in copies:
        cp.wait()


def local(
    rows_in, norm_gain, w_query, w_keyval, w_out, page_pool, stretch_ids, page_slot, picked, question_len
):
    any_spec = pl.BlockSpec(memory_space=pl.ANY)
    vmem = pl.BlockSpec(memory_space=pltpu.VMEM)
    sem = pltpu.SemaphoreType.DMA
    attn, joined = pl.pallas_call(
        kernel,
        out_shape=(pltpu.VMEM((1, ROWS, 2 * HD), BF16), pltpu.VMEM(page_pool.shape, BF16)),
        in_specs=[any_spec] * 10,
        out_specs=(vmem, vmem),
        scratch_shapes=[
            pltpu.SMEM((4, SPANS), jnp.int32),
            pltpu.SMEM((32,), jnp.int32),
            pltpu.VMEM((4, SPANS, RCH), jnp.int32),
            pltpu.SMEM((4,), jnp.int32),
            pltpu.VMEM((ROWS, D), BF16),
            pltpu.VMEM((1, D), F32),
            pltpu.VMEM((ROWS, D), BF16),
            pltpu.VMEM((D, 2 * HD), BF16),
            pltpu.VMEM((HD, D), BF16),
            pltpu.VMEM((D, 2 * HD), BF16),
            pltpu.VMEM((8, 16, 2048), BF16),
            pltpu.VMEM((4, KVH, 2, 16, HD), BF16),
            pltpu.VMEM((2, 64, 2, 16, HD), BF16),
            pltpu.VMEM((ROWS, HD), BF16),
            pltpu.VMEM((4, ROWS, HD), BF16),
            pltpu.VMEM((2, 256, HD), BF16),
            pltpu.VMEM((2 * ROWS, HD), BF16),
            pltpu.VMEM((9, 2 * ROWS, 256), F32),
            pltpu.VMEM((2 * ROWS, 128), F32),
            pltpu.VMEM((2, 16, ROWS, 2 * HD), BF16),
            pltpu.VMEM((ROWS, 2 * HD), F32),
            pltpu.VMEM((4, 2 * RCH, HD), BF16),
            pltpu.VMEM((2, 2 * RCH, HD), BF16),
            pltpu.VMEM((2, KVH, 2, 2 * RCH, HD), BF16),
            sem((21,)),
            sem((1,)),
            sem((4,)),
            sem((1,)),
            sem((4,)),
            sem((2,)),
            sem((2,)),
            sem((1,)),
            sem((2,)),
            sem((2,)),
            sem((2,)),
            sem((1,)),
            sem((16,)),
            sem((1,)),
            sem((16,)),
        ],
        compiler_params=pltpu.CompilerParams(
            collective_id=0, has_side_effects=True, vmem_limit_bytes=56 * 1024 * 1024
        ),
        name="joined_attention",
    )(
        rows_in,
        norm_gain.reshape(1, D),
        w_query,
        w_keyval.T,
        w_out,
        page_pool,
        stretch_ids,
        page_slot,
        picked,
        question_len,
    )
    return pl.pallas_call(
        finish,
        out_shape=(
            jax.ShapeDtypeStruct(attn.shape, BF16),
            jax.ShapeDtypeStruct(joined.shape, BF16),
        ),
        in_specs=[vmem, vmem],
        out_specs=(any_spec, any_spec),
        scratch_shapes=[sem((2,))],
        name="write_out",
    )(pltpu.with_memory_space_constraint(attn, pltpu.VMEM), pltpu.with_memory_space_constraint(joined, pltpu.VMEM))


def solution(mesh):
    in_specs = (
        P("req", None, None),
        P(),
        P(None, "grp"),
        P(None, "grp"),
        P(None, "grp"),
        P("req", "grp", None),
        P(),
        P(),
        P(),
        P(),
    )
    out_specs = (P("req", None, "grp"), P("req", "grp", None))
    return jax.shard_map(local, mesh=mesh, in_specs=in_specs, out_specs=out_specs, check_vma=False)
```

```python
import functools
import math

import jax
import jax.numpy as jnp
from jax import lax
from jax.experimental import pallas as pl
from jax.experimental.pallas import tpu as pltpu
from jax.sharding import PartitionSpec as P

MESH = pl.DeviceIdType.MESH
F32 = jnp.float32
BF16 = jnp.bfloat16
HD = 128
KVH = 8
ROWS = 160
RCH = 24
SPANS = 4
D = 8192
KEYS = 2048
EPS = 1e-05
EXP2_SCALE = math.log2(math.e) / math.sqrt(HD)
NEG = -1e30
FAR = 1e9
LINE = (0, 1, 3, 2)
HOPS = (0, 1, 2, 1)
NEAREST_FIRST = sorted(
    [(n // 16, n // 4 % 4, n % 4) for n in range(1, 64)], key=lambda steps: sum(HOPS[d] for d in steps)
)


def nt_dot(a, b):
    return lax.dot_general(a, b, (((1,), (1,)), ((), ())), preferred_element_type=F32)


def nn_dot(a, b):
    return jnp.dot(a, b, preferred_element_type=F32)


def by_index(index, values):
    low = jnp.where(index == 0, values[0], values[1])
    return jnp.where(index < 2, low, jnp.where(index == 2, values[2], values[3]))


def to_column(row):
    n = row.shape[1]
    eye = lax.broadcasted_iota(jnp.int32, (n, n), 0) == lax.broadcasted_iota(jnp.int32, (n, n), 1)
    return jnp.sum(jnp.where(eye, jnp.broadcast_to(row, (n, n)), 0.0), axis=1, keepdims=True)


def kernel(
    rows_hbm,
    gain_hbm,
    wq_hbm,
    wk_hbm,
    wo_hbm,
    pool_hbm,
    ids_hbm,
    slots_hbm,
    picked_hbm,
    qlen_hbm,
    out_ref,
    joined_v,
    ids,
    slots,
    picked,
    qlen,
    rows_v,
    gain_v,
    nrm,
    wq_v,
    wk_v,
    wo_v,
    pool_v,
    sx,
    kv,
    kvp,
    fr,
    fk,
    q2,
    scores,
    peak,
    gath,
    acc,
    sj,
    rj1,
    rj,
    ld,
    zs_s,
    zs_r,
    cs_s,
    cs_r,
    fr_s,
    fr_r,
    js_s,
    js_r,
    jz_s,
    jz_r,
    g_s,
    g_r,
    gc_s,
    gc_r,
):
    r = lax.axis_index("req")
    m = lax.axis_index("grp")
    z = lax.div(m, 8)
    y = lax.rem(lax.div(m, 2), 4)
    c = lax.rem(m, 2)
    chip = lax.div(m, 2)
    k = lax.div(m, 4)
    sib = (r, m + 1 - 2 * c)

    def load(src, dst, i):
        cp = pltpu.make_async_copy(src, dst, ld.at[i])
        cp.start()
        return cp

    def push(src, dst, send, recv, dev):
        pltpu.make_async_remote_copy(
            src_ref=src, dst_ref=dst, send_sem=send, recv_sem=recv, device_id=dev, device_id_type=MESH
        ).start()

    def wait_all(ref, sem):
        pltpu.make_async_copy(ref, ref, sem).wait()

    barrier = pltpu.get_barrier_semaphore()

    def others(act, first=0, last=63):
        for dx, dy, dz in NEAREST_FIRST[first:last]:
            act(lax.rem(r + dx, 4), 4 * lax.rem(z + dz, 4) + lax.rem(y + dy, 4))

    def greet(q, t):
        pl.semaphore_signal(barrier, inc=1, device_id=(q, 2 * t + c), device_id_type=MESH)

    others(greet)
    pl.semaphore_signal(barrier, inc=1, device_id=sib, device_id_type=MESH)

    ld_small = [
        load(ids_hbm, ids, 17),
        load(slots_hbm, slots, 18),
        load(qlen_hbm, qlen, 19),
        load(picked_hbm, picked, 20),
    ]
    for i in range(5):
        load(rows_hbm.at[0, pl.ds(32 * i, 32)], rows_v.at[pl.ds(32 * i, 32)], 1 + i)
    ld_gain = load(gain_hbm, gain_v, 6)
    ld_pool = load(pool_hbm, pool_v, 0)
    ld_wk = load(wk_hbm, wk_v.at[pl.ds(pl.multiple_of(64 * c, 64), 64)], 7)
    ld_wq = [
        load(wq_hbm.at[pl.ds(1024 * i, 1024)], wq_v.at[pl.ds(1024 * i, 1024)], 8 + i) for i in range(8)
    ]

    wk_v[pl.ds(pl.multiple_of(64 - 64 * c, 64), 64), :] = jnp.zeros((64, D), BF16)

    for cp in ld_small:
        cp.wait()
    place = [[slots[ids[q, s]] for s in range(SPANS)] for q in range(4)]
    send_slot, send_span = [], []
    for q in range(4):
        slot_q, span_q = 0, 0
        for s in range(SPANS):
            here = (place[q][s] >> 3) == r
            slot_q = slot_q + jnp.where(here, place[q][s] & 7, 0)
            span_q = span_q + jnp.where(here, s, 0)
        send_slot.append(slot_q)
        send_span.append(span_q)
    own_place = [slots[ids[r, s]] for s in range(SPANS)]
    span_of = []
    for x in range(4):
        span_x = 0
        for s in range(SPANS):
            span_x = span_x + jnp.where((own_place[s] >> 3) == x, s, 0)
        span_of.append(span_x)

    ld_pool.wait()
    row = lax.broadcasted_iota(jnp.int32, (64, 128), 0)
    wanted = by_index(row >> 4, send_slot) * 16 + (row & 15)
    pick_page = jnp.where(lax.broadcasted_iota(jnp.int32, (64, 128), 1) == wanted, 1.0, 0.0).astype(BF16)
    for h in range(2 * KVH):
        piece = nn_dot(pick_page, pool_v[:, :, h * HD : (h + 1) * HD].reshape(128, HD)).astype(BF16)
        for q in range(4):
            sx[q, h % KVH, h // KVH] = piece[16 * q : 16 * (q + 1)]
    ld_gain.wait()

    def norm(i, carry):
        at = pl.ds(pl.multiple_of(32 * i, 32), 32)
        wait_all(rows_v.at[at], ld.at[1 + i])
        squares = jnp.zeros((32, 128), F32)
        for j in range(D // 128):
            v = rows_v[at, j * 128 : (j + 1) * 128].astype(F32)
            squares = squares + v * v
        mean = jnp.sum(squares, axis=1, keepdims=True) * (1.0 / D)
        inv = jnp.broadcast_to(lax.rsqrt(mean + EPS), (32, 128))
        for j in range(D // 128):
            v = rows_v[at, j * 128 : (j + 1) * 128].astype(F32)
            nrm[at, j * 128 : (j + 1) * 128] = (v * inv * gain_v[:, j * 128 : (j + 1) * 128]).astype(BF16)
        return carry

    lax.fori_loop(0, 5, norm, 0)


    ld_wk.wait()
    new_kv = jnp.zeros((ROWS, HD), F32)
    for i in range(8):
        cols = slice(1024 * i, 1024 * (i + 1))
        new_kv = new_kv + nt_dot(nrm[:, cols], wk_v[:, cols])
    kvp[...] = new_kv.astype(BF16)
    pl.semaphore_wait(barrier, 64)
    head_to = lax.div(lax.rem(m, 16), 2)
    fr_slot = 2 * c + lax.div(m, 16)
    for i in range(2):
        t = 2 * head_to + i

        @pl.when(t == chip)
        def _():
            pltpu.make_async_copy(kvp, fr.at[fr_slot], fr_r.at[0]).start()

        @pl.when(t != chip)
        def _():
            push(kvp, fr.at[fr_slot], fr_s.at[0], fr_r.at[0], (r, 2 * t + c))

    def send_page(q, t):
        push(sx.at[q, lax.div(t, 2)], kv.at[c, 16 * r + chip], zs_s.at[0], zs_r.at[r], (q, 2 * t + c))

    pltpu.make_async_copy(sx.at[r, k], kv.at[c, 16 * r + chip], zs_r.at[r]).start()

    pl.when(m >= 0)(functools.partial(others, send_page))
    query = jnp.zeros((ROWS, 2 * HD), F32)
    for i in range(8):
        ld_wq[i].wait()
        at = slice(1024 * i, 1024 * (i + 1))
        query = query + nn_dot(nrm[:, at], wq_v[at, :])
    q2[0:ROWS, :] = query[:, 0:HD].astype(BF16)
    q2[ROWS : 2 * ROWS, :] = query[:, HD : 2 * HD].astype(BF16)

    own_half = fr.at[pl.ds(2 * c, 2)]
    wait_all(own_half, fr_r.at[0])
    push(own_half, own_half, fr_s.at[1], fr_r.at[1], sib)

    own_picked = picked[r].astype(F32)
    cols = [to_column(own_picked[s : s + 1, :]) + 512.0 * s for s in range(SPANS)]
    question = lax.broadcasted_iota(jnp.int32, (64, 1), 0).astype(F32)
    own_len = qlen[r].astype(F32)
    row_pos = jnp.concatenate(cols + [question + float(KEYS)], axis=0)
    key_col = jnp.concatenate(cols + [jnp.where(question < own_len, question + float(KEYS), FAR)], axis=0)
    eye = lax.broadcasted_iota(jnp.int32, (ROWS, 256), 0) == lax.broadcasted_iota(jnp.int32, (ROWS, 256), 1)
    fresh_pos = jnp.sum(jnp.where(eye, jnp.broadcast_to(key_col, (ROWS, 256)), 0.0), axis=0, keepdims=True)
    fresh_pos = jnp.where(lax.broadcasted_iota(jnp.int32, (1, 256), 1) < ROWS, fresh_pos, FAR)
    row_pos_b = jnp.broadcast_to(row_pos, (ROWS, 256))
    picked_b = row_pos_b[0 : SPANS * RCH]

    wait_all(fr.at[pl.ds(2 - 2 * c, 2)], fr_r.at[1])
    row = lax.broadcasted_iota(jnp.int32, (SPANS * RCH, 256), 0)
    wanted = by_index(lax.div(row, RCH), span_of) * RCH + lax.rem(row, RCH)
    pick_rows = jnp.where(lax.broadcasted_iota(jnp.int32, (SPANS * RCH, 256), 1) == wanted, 1.0, 0.0).astype(BF16)
    by_holder = []
    for s in range(2):
        fk[s, 0:ROWS, :] = (fr[s].astype(F32) + fr[2 + s].astype(F32)).astype(BF16)
        fk[s, ROWS:256, :] = jnp.zeros((256 - ROWS, HD), BF16)
        by_holder.append(nn_dot(pick_rows, fk[s]))
    for x in range(4):
        sj[x] = jnp.concatenate([b[x * RCH : (x + 1) * RCH] for b in by_holder], axis=0).astype(BF16)
    rj_half = lax.div(r, 2)
    rj_slot = lax.rem(r, 2)

    @pl.when(rj_half == c)
    def _():
        for d in (2, 1, 3):
            x = lax.rem(r + d, 4)
            push(sj.at[x], rj1.at[rj_slot], js_s.at[0], js_r.at[rj_slot], (x, m))
        rj1[rj_slot] = sj[r]

    def score(at, keys, key_pos):
        s = nt_dot(q2[...], keys)
        seen = row_pos_b >= jnp.broadcast_to(key_pos, (ROWS, 256))
        for half in range(2):
            rows = slice(half * ROWS, (half + 1) * ROWS)
            masked = jnp.where(seen, s[rows], NEG)
            scores[at, rows, :] = masked
            peak[rows, :] = jnp.maximum(peak[rows, :], jnp.maximum(masked[:, :128], masked[:, 128:]))

    peak[...] = jnp.full((2 * ROWS, 128), NEG, F32)
    score(8, fk[0], fresh_pos)

    def group(cc, x):
        return kv.at[cc, pl.ds(16 * x, 16)]

    for d in (2, 1, 3, 0):
        x = lax.rem(r + d, 4)
        wait_all(group(c, x), zs_r.at[x])
        push(group(c, x), group(c, x), cs_s.at[0], cs_r.at[x], sib)

    for q in range(2):

        @pl.when(r != 2 * c + q)
        def _():
            wait_all(rj1.at[q], js_r.at[q])

    rj[c, k] = rj1[...]

    def spread_fresh(d, carry):
        t = lax.rem(k + d, 8)
        push(rj1, rj.at[c, k], jz_s.at[0], jz_r.at[0], (r, (2 * t + lax.rem(y, 2)) * 2 + c))
        return carry

    lax.fori_loop(1, 8, spread_fresh, 0)

    ld_wo = load(wo_hbm, wo_v, 16)
    lane = lax.broadcasted_iota(jnp.int32, (1, 256), 1)
    lane_pos = (lane >> 4) * 32 + (lane & 15)

    def page_keys(cc, x):
        span = jnp.where(x == 0, span_of[0], jnp.where(x == 1, span_of[1], jnp.where(x == 2, span_of[2], span_of[3])))
        pos = (lane_pos + (span * 512 + cc * 16)).astype(F32)
        same = picked_b == jnp.broadcast_to(pos, (SPANS * RCH, 256))
        gone = jnp.max(jnp.where(same, 1.0, 0.0), axis=0, keepdims=True)
        return jnp.where(gone > 0.5, FAR, pos)

    def page_part(cc, x, s):
        return kv[cc, pl.ds(16 * x, 16), s].reshape(256, HD)

    for x in range(4):
        score(4 * c + x, page_part(c, x, 0), page_keys(c, x))

    for x in range(4):
        wait_all(group(1 - c, x), cs_r.at[x])
        score(4 * (1 - c) + x, page_part(1 - c, x, 0), page_keys(1 - c, x))

    for h in range(2):
        rows = slice(h * ROWS, (h + 1) * ROWS)
        top = jnp.broadcast_to(jnp.max(peak[rows, :], axis=1, keepdims=True), (ROWS, 128))
        total = jnp.zeros((ROWS, 128), F32)
        mixed = jnp.zeros((ROWS, HD), F32)
        for i in range(9):
            w0 = jnp.exp2((scores[i, rows, 0:128] - top) * EXP2_SCALE)
            w1 = jnp.exp2((scores[i, rows, 128:256] - top) * EXP2_SCALE)
            total = total + (w0 + w1)
            vals = fk[1] if i == 8 else page_part(i // 4, i % 4, 1)
            mixed = mixed + nn_dot(jnp.concatenate([w0, w1], axis=1).astype(BF16), vals)
        att = mixed / jnp.sum(total, axis=1, keepdims=True)
        gath[c, chip, :, h * HD : (h + 1) * HD] = att.astype(BF16)

    def chip_at(cc, df, ds):
        f = lax.rem(y * (1 - cc) + z * cc + df, 4)
        s = lax.rem(z * (1 - cc) + y * cc + ds, 4)
        return (4 * s + f) * (1 - cc) + (4 * f + s) * cc

    def forward(block, df, ds):
        ref = gath.at[c, block]
        push(ref, ref, g_s.at[0], g_r.at[block], (r, 2 * chip_at(c, df, ds) + c))

    def across(block):
        ref = gath.at[c, block]
        push(ref, ref, gc_s.at[0], gc_r.at[block], sib)

    def arrived(block):
        wait_all(gath.at[c, block], g_r.at[block])

    def project(cc, ds):
        more = jnp.zeros((ROWS, 2 * HD), F32)
        for df in LINE:
            block = chip_at(cc, df, ds)
            at = pl.multiple_of((2 * block + cc) * 256, 256)
            more = more + nn_dot(gath[cc, block], wo_v[pl.ds(at, 256), :])
        acc[...] += more

    def crossed(ds):
        for df in LINE:
            block = chip_at(1 - c, df, ds)
            wait_all(gath.at[1 - c, block], gc_r.at[block])

    for df in (1, 3, 2):
        forward(chip, df, 0)
    across(chip)
    for ds in (1, 3):
        forward(chip, 0, ds)
    acc[...] = jnp.zeros((ROWS, 2 * HD), F32)
    for df in (1, 3, 2):
        block = chip_at(c, df, 0)
        arrived(block)
        for ds in (2, 1, 3) if df == 2 else (1, 3):
            forward(block, 0, ds)
        across(block)
    ld_wo.wait()
    project(c, 0)
    for df, ds in ((0, 1), (0, 3), (1, 3), (3, 1), (1, 1), (3, 3), (2, 1), (2, 3), (0, 2)):
        block = chip_at(c, df, ds)
        arrived(block)
        if (df, ds) in ((0, 1), (1, 3), (3, 1)):
            forward(block, 0, 4 - ds)
        across(block)
    crossed(0)
    wait_all(rj.at[c, pl.ds(0, 7)], jz_r.at[0])
    push(rj.at[c], rj.at[c], jz_s.at[1], jz_r.at[1], sib)
    project(1 - c, 0)
    project(c, 1)
    project(c, 3)

    crossed(1)
    project(1 - c, 1)
    crossed(3)
    project(1 - c, 3)
    for df in (2, 1, 3):
        block = chip_at(c, df, 2)
        arrived(block)
        across(block)
    project(c, 2)
    wait_all(rj.at[1 - c], jz_r.at[1])
    col = lax.broadcasted_iota(jnp.int32, (RCH, 192), 1)
    col_req = lax.div(col, 48)
    col_in = lax.rem(col, 48)
    row_in = lax.broadcasted_iota(jnp.int32, (RCH, 192), 0)
    target = jnp.zeros((1, 192), F32)
    low = (m * 16).astype(F32)
    for q in range(4):
        pq = picked[q].astype(F32)
        mine = jnp.zeros((1, RCH), F32)
        for s in range(SPANS):
            mine = mine + jnp.where(send_span[q] == s, pq[s : s + 1, :], 0.0)
        mine = mine - low
        mine = jnp.where((mine >= 0.0) & (mine < 16.0), mine + (send_slot[q] * 16).astype(F32), -1.0)
        fits = (col_req == q) & ((col_in == row_in) | (col_in == row_in + RCH))
        target = target + jnp.sum(
            jnp.where(fits, jnp.broadcast_to(to_column(mine), (RCH, 192)), 0.0), axis=0, keepdims=True
        )
    line = lax.broadcasted_iota(jnp.int32, (128, 192), 0).astype(F32)
    is_key = lax.rem(lax.broadcasted_iota(jnp.int32, (128, 192), 1), 48) < RCH
    match = line == jnp.broadcast_to(target, (128, 192))
    pick_key = jnp.where(match & is_key, 1.0, 0.0)
    pick_val = jnp.where(match & jnp.logical_not(is_key), 1.0, 0.0)
    hit = jnp.broadcast_to(jnp.max(pick_key, axis=1, keepdims=True), (128, HD)) > 0.5
    pick = jnp.concatenate([pick_key, pick_val], axis=0).astype(BF16)
    for h in range(KVH):
        new = nn_dot(pick[:, 0:96], rj[0, h].reshape(96, HD)) + nn_dot(pick[:, 96:192], rj[1, h].reshape(96, HD))
        for s in range(2):
            at = slice(1024 * s + h * HD, 1024 * s + (h + 1) * HD)
            old = pool_v[:, :, at].astype(F32).reshape(128, HD)
            joined_v[:, :, at] = (
                jnp.where(hit, new[128 * s : 128 * (s + 1)], old).astype(BF16).reshape(8, 16, HD)
            )

    crossed(2)
    project(1 - c, 2)
    live = lax.broadcasted_iota(jnp.int32, (ROWS, 2 * HD), 0) < SPANS * RCH + qlen[r]
    out_ref[0] = jnp.where(live, acc[...], 0.0).astype(BF16)

    wait_all(kv.at[0, pl.ds(0, 63)], zs_s.at[0])
    wait_all(kv.at[0], cs_s.at[0])

    wait_all(own_half, fr_s.at[1])

    @pl.when(head_to == k)
    def _():
        wait_all(fr.at[pl.ds(0, 1)], fr_s.at[0])

    @pl.when(head_to != k)
    def _():
        wait_all(fr.at[pl.ds(0, 2)], fr_s.at[0])


    @pl.when(rj_half == c)
    def _():
        wait_all(sj.at[pl.ds(0, 3)], js_s.at[0])

    wait_all(rj.at[0, pl.ds(0, 7)], jz_s.at[0])
    wait_all(rj.at[0], jz_s.at[1])
    wait_all(gath.at[0, pl.ds(0, 15)], g_s.at[0])
    wait_all(gath.at[0], gc_s.at[0])


def finish(attn, joined, attn_out, joined_out, sems):
    copies = [
        pltpu.make_async_copy(joined, joined_out, sems.at[0]),
        pltpu.make_async_copy(attn, attn_out, sems.at[1]),
    ]
    for cp in copies:
        cp.start()
    for cp in copies:
        cp.wait()


def local(
    rows_in, norm_gain, w_query, w_keyval, w_out, page_pool, stretch_ids, page_slot, picked, question_len
):
    any_spec = pl.BlockSpec(memory_space=pl.ANY)
    vmem = pl.BlockSpec(memory_space=pltpu.VMEM)
    sem = pltpu.SemaphoreType.DMA
    attn, joined = pl.pallas_call(
        kernel,
        out_shape=(pltpu.VMEM((1, ROWS, 2 * HD), BF16), pltpu.VMEM(page_pool.shape, BF16)),
        in_specs=[any_spec] * 10,
        out_specs=(vmem, vmem),
        scratch_shapes=[
            pltpu.SMEM((4, SPANS), jnp.int32),
            pltpu.SMEM((32,), jnp.int32),
            pltpu.VMEM((4, SPANS, RCH), jnp.int32),
            pltpu.SMEM((4,), jnp.int32),
            pltpu.VMEM((ROWS, D), BF16),
            pltpu.VMEM((1, D), F32),
            pltpu.VMEM((ROWS, D), BF16),
            pltpu.VMEM((D, 2 * HD), BF16),
            pltpu.VMEM((HD, D), BF16),
            pltpu.VMEM((D, 2 * HD), BF16),
            pltpu.VMEM((8, 16, 2048), BF16),
            pltpu.VMEM((4, KVH, 2, 16, HD), BF16),
            pltpu.VMEM((2, 64, 2, 16, HD), BF16),
            pltpu.VMEM((ROWS, HD), BF16),
            pltpu.VMEM((4, ROWS, HD), BF16),
            pltpu.VMEM((2, 256, HD), BF16),
            pltpu.VMEM((2 * ROWS, HD), BF16),
            pltpu.VMEM((9, 2 * ROWS, 256), F32),
            pltpu.VMEM((2 * ROWS, 128), F32),
            pltpu.VMEM((2, 16, ROWS, 2 * HD), BF16),
            pltpu.VMEM((ROWS, 2 * HD), F32),
            pltpu.VMEM((4, 2 * RCH, HD), BF16),
            pltpu.VMEM((2, 2 * RCH, HD), BF16),
            pltpu.VMEM((2, KVH, 2, 2 * RCH, HD), BF16),
            sem((21,)),
            sem((1,)),
            sem((4,)),
            sem((1,)),
            sem((4,)),
            sem((2,)),
            sem((2,)),
            sem((1,)),
            sem((2,)),
            sem((2,)),
            sem((2,)),
            sem((1,)),
            sem((16,)),
            sem((1,)),
            sem((16,)),
        ],
        compiler_params=pltpu.CompilerParams(
            collective_id=0, has_side_effects=True, vmem_limit_bytes=56 * 1024 * 1024
        ),
        name="joined_attention",
    )(
        rows_in,
        norm_gain.reshape(1, D),
        w_query,
        w_keyval.T,
        w_out,
        page_pool,
        stretch_ids,
        page_slot,
        picked,
        question_len,
    )
    return pl.pallas_call(
        finish,
        out_shape=(
            jax.ShapeDtypeStruct(attn.shape, BF16),
            jax.ShapeDtypeStruct(joined.shape, BF16),
        ),
        in_specs=[vmem, vmem],
        out_specs=(any_spec, any_spec),
        scratch_shapes=[sem((2,))],
        name="write_out",
    )(pltpu.with_memory_space_constraint(attn, pltpu.VMEM), pltpu.with_memory_space_constraint(joined, pltpu.VMEM))


def solution(mesh):
    in_specs = (
        P("req", None, None),
        P(),
        P(None, "grp"),
        P(None, "grp"),
        P(None, "grp"),
        P("req", "grp", None),
        P(),
        P(),
        P(),
        P(),
    )
    out_specs = (P("req", None, "grp"), P("req", "grp", None))
    return jax.shard_map(local, mesh=mesh, in_specs=in_specs, out_specs=out_specs, check_vma=False)
```
